256 devices in a mesh: ctx: 32 (over z, y_hi, core), tp: 8 (over x, y_lo).
Axes of the slice: x: 4, y: 4 (y_hi: 2, y_lo: 2; y = y_hi * 2 + y_lo), z: 8, core: 2. Of those that a mesh axis runs over, the one named last changes fastest.
Arguments:
- hidden_states: bfloat16 [8192, 4096], P('ctx', 'tp'), may hold values from -40 to 40
- w_query: bfloat16 [4096, 4096], P(None, 'tp'), may hold values from -0.25 to 0.25
- w_key: bfloat16 [4096, 1024], P(None, 'tp'), may hold values from -0.5 to 0.5
- w_value: bfloat16 [4096, 1024], P(None, 'tp'), may hold values from -0.09375 to 0.09375
- w_out: bfloat16 [4096, 4096], P('tp'), may hold values from -0.09375 to 0.09375
- span_order: int32 [64], replicated, may hold values from 0 to 63, each once
- lengths: int32 [4], replicated, may hold values from 1 to 4096, 8192 in all
Outputs:
- attention_out: bfloat16 [8192, 4096], P('ctx', 'tp')
The draws below stay inside these ranges and needn't reach their ends.
Inputs may be any that keep to these rules, and one draw needn't show every extreme that they name: `span_order`: each value appears exactly once. `lengths`: they sum to 8192; the longest is exactly 4096.
All inputs are finite; a program needn't handle non-finite values.
Results may differ from the reference program's by a relative error of at most 0.02.
Values may be sent and summed in bfloat16 or wider, within the bound.
No kernel may reach another device: no remote copies, remote signals or barrier semaphores. Data moves between devices by JAX's collectives and lax.ppermute only.
A program may use at most 64 MiB of HBM per device.

```python
import math
import jax
import jax.numpy as jnp
import numpy as np
from jax import lax

D = 4096
HEADS = 32
KV_HEADS = 8
HEAD_DIM = 128
ROLLOUTS = 4
SPAN = 128
SEQ = 8192
N_CTX = 32
N_TP = 8


def query_weights(key):
    return jax.random.normal(key, (D, HEADS * HEAD_DIM), jnp.float32) / math.sqrt(D)


def draw_w_query(key, part):
    shared = query_weights(key)
    return jnp.clip(shared, -0.25, 0.25).astype(jnp.bfloat16)


def draw_w_key(key, part):
    key = jax.random.fold_in(key, 11)
    noise = jax.random.normal(key, (D, KV_HEADS * HEAD_DIM), jnp.float32) / math.sqrt(D)
    result = noise
    return jnp.clip(result, -0.5, 0.5).astype(jnp.bfloat16)


def draw_hidden_states(key, part):
    key = jax.random.fold_in(key, 3)
    first_key = jax.random.fold_in(key, 0)
    base = jax.random.normal(first_key, (SEQ, D), jnp.float32)
    result = jnp.clip(base, -6.0, 6.0)
    return result.astype(jnp.bfloat16)


def block_scale(key, shape, cuts, smallest, largest):
    gain, own = 1.0, jax.random.fold_in(key, 6)
    for position, shards_of in cuts:
        draws = jnp.exp(jax.random.uniform(jax.random.fold_in(own, position), (shards_of,), jnp.float32, smallest / len(cuts), largest / len(cuts)))
        gain = gain * jnp.repeat(draws, shape[position] // shards_of).reshape([-1 if axis == position else 1 for axis in range(len(shape))])
    return gain


def split_up(number_of, total, most, skew):
    loads = [(1 << 20) // math.isqrt(standing ** skew) + 1 for standing in range(2, number_of + 1)]
    rest, counts = total - most - (number_of - 1), [1] * (number_of - 1)
    while rest > 0:
        candidates = [i for i in range(number_of - 1) if counts[i] < most]
        mass, budget = sum([loads[i] for i in candidates]), rest
        for i in candidates:
            extra = min(most - counts[i], max(1, budget * loads[i] // mass), rest)
            counts[i] = counts[i] + extra
            rest = rest - extra
    return np.array([most] + counts)


def uneven_parts(rng, number_of, total, bound, slope):
    if number_of == 2:
        one = jax.random.randint(rng, (), max(1, total - bound), min(bound, total - 1) + 1)
        return jnp.stack([one, total - one])
    tallies = jnp.asarray(split_up(number_of, total, bound, slope), jnp.int32)
    couples = (number_of - 1) // 2
    giver, taker = tallies[1:1 + 2 * couples:2], tallies[2:2 + 2 * couples:2]
    margin = jnp.minimum(giver - 1, bound - taker)
    passed = jax.random.randint(jax.random.fold_in(rng, 1), (couples,), 0, 1 << 20) % (margin + 1)
    tallies = tallies.at[1:1 + 2 * couples:2].set(giver - passed).at[2:2 + 2 * couples:2].set(taker + passed)
    return tallies[jax.random.permutation(jax.random.fold_in(rng, 2), number_of)]


def gaussian(rng, shape, scale, most, cuts=(), kind=jnp.bfloat16):
    values = scale * jax.random.normal(rng, shape, jnp.float32)
    if cuts:
        values = values * block_scale(rng, shape, cuts, -0.22, 0.18)
    return jnp.clip(values, -most, most).astype(kind)


def setup_inputs(seed: int = 0) -> dict:
    splits = jax.random.split(jax.random.key(seed), 8)
    hidden_states = draw_hidden_states(jax.random.fold_in(splits[7], 71), 0)
    w_query = draw_w_query(jax.random.fold_in(splits[7], 71), 0)
    w_key = draw_w_key(jax.random.fold_in(splits[7], 71), 0)
    w_value = gaussian(splits[3], (D, KV_HEADS * HEAD_DIM), D ** -0.5, 0.09375, ((1, 8),))
    w_out = gaussian(splits[4], (HEADS * HEAD_DIM, D), (HEADS * HEAD_DIM) ** -0.5, 0.09375, ((0, 8),))
    span_order = jax.random.permutation(splits[5], 2 * N_CTX).astype(jnp.int32)
    lengths = uneven_parts(splits[6], ROLLOUTS, SEQ, SEQ // 2, 2).astype(jnp.int32)
    return {"hidden_states": hidden_states, "w_query": w_query, "w_key": w_key, "w_value": w_value, "w_out": w_out, "span_order": span_order, "lengths": lengths}


ROPE_BASE = 500000.0
NEG_FILL = -1e+30

def rotate_half(values, positions):
    head_dim = values.shape[-1]
    half_dim = head_dim // 2
    exponent = jnp.arange(half_dim, dtype=jnp.float32) * (2.0 / head_dim)
    frequency = jnp.power(jnp.float32(ROPE_BASE), -exponent)
    angles = positions.astype(jnp.float32)[:, None] * frequency[None, :]
    cosine = jnp.cos(angles)[:, None, :]
    sine_part = jnp.sin(angles)[:, None, :]
    lower_half = values[..., :half_dim]
    upper_half = values[..., half_dim:]
    return jnp.concatenate([lower_half * cosine - upper_half * sine_part, upper_half * cosine + lower_half * sine_part], axis=-1)

def reference(hidden_states, w_query, w_key, w_value, w_out, span_order, lengths):
    offsets = jnp.arange(SPAN, dtype=jnp.int32)
    positions = (span_order.astype(jnp.int32)[:, None] * SPAN + offsets[None, :]).reshape(SEQ)
    boundaries = jnp.cumsum(lengths).astype(jnp.int32)[:-1]
    segments = lax.optimization_barrier(jnp.sum((positions[:, None] >= boundaries[None, :]).astype(jnp.int32), axis=1))
    queries = jnp.dot(hidden_states, w_query, preferred_element_type=jnp.float32).reshape(SEQ, HEADS, HEAD_DIM)
    keys_raw = jnp.dot(hidden_states, w_key, preferred_element_type=jnp.float32).reshape(SEQ, KV_HEADS, HEAD_DIM)
    values_raw = jnp.dot(hidden_states, w_value, preferred_element_type=jnp.float32).reshape(SEQ, KV_HEADS, HEAD_DIM)
    q_rot = rotate_half(queries, positions).astype(jnp.bfloat16)
    k_rot = rotate_half(keys_raw, positions).astype(jnp.bfloat16)
    v_all = values_raw.astype(jnp.bfloat16)
    group_size = HEADS // KV_HEADS
    score_scale = 1.0 / math.sqrt(HEAD_DIM)
    block_rows = math.gcd(SEQ, 256)
    block_count = SEQ // block_rows
    keys_f = k_rot.astype(jnp.float32).transpose(1, 0, 2)
    values_f = v_all.astype(jnp.float32).transpose(1, 0, 2)
    queries_f = q_rot.astype(jnp.float32).reshape(block_count, block_rows, KV_HEADS, group_size, HEAD_DIM)

    def one_block(operands):
        query_block, query_pos, query_seg = operands
        allowed = (positions[None, :] <= query_pos[:, None]) & (segments[None, :] == query_seg[:, None])

        def one_head(head_operands):
            query_head, key_head, value_head = head_operands
            scores = jnp.einsum('rgd,nd->grn', query_head, key_head, precision=lax.Precision.HIGHEST) * score_scale
            masked = jnp.where(allowed[None], scores, NEG_FILL)
            highest = lax.optimization_barrier(jnp.max(masked, axis=-1))
            weights = jnp.where(allowed[None], jnp.exp(scores - highest[..., None]), 0.0)
            totals = lax.optimization_barrier(jnp.sum(weights, axis=-1))
            weights_b = lax.optimization_barrier(weights.astype(jnp.bfloat16)).astype(jnp.float32)
            summed = jnp.einsum('grn,nd->grd', weights_b, value_head, precision=lax.Precision.HIGHEST)
            return summed / totals[..., None]
        per_head = lax.map(one_head, (query_block.transpose(1, 0, 2, 3), keys_f, values_f))
        return per_head.transpose(2, 0, 1, 3).reshape(block_rows, HEADS * HEAD_DIM).astype(jnp.bfloat16)
    context = lax.map(one_block, (queries_f, positions.reshape(block_count, block_rows), segments.reshape(block_count, block_rows)))
    context = context.reshape(SEQ, HEADS * HEAD_DIM)
    group_cols = HEADS * HEAD_DIM // N_TP
    summed_out = jnp.zeros((SEQ, D), jnp.float32)
    for group_index in range(N_TP):
        cols = context[:, group_index * group_cols:(group_index + 1) * group_cols]
        rows = w_out[group_index * group_cols:(group_index + 1) * group_cols]
        partial_value = jnp.dot(cols, rows, preferred_element_type=jnp.float32)
        partial_value = lax.optimization_barrier(partial_value.astype(jnp.bfloat16)).astype(jnp.float32)
        summed_out = summed_out + partial_value
    return summed_out.astype(jnp.bfloat16)
```

```python
import functools
import math

import jax
import jax.numpy as jnp
from jax import lax
from jax.experimental import pallas as pl
from jax.experimental.pallas import tpu as pltpu
from jax.sharding import PartitionSpec as P

HEADS = 32
KV_HEADS = 8
HEAD_DIM = 128
GROUP = HEADS // KV_HEADS
SPAN = 128
SEQ = 8192
D = 4096
N_CTX = 32
N_TP = 8
FEATS = D // N_TP
ROWS = SEQ // N_CTX
BLOCKS = SEQ // SPAN
STEP = 4

ROPE_BASE = 500000.0
MASKED = -1e30
LOWEST = -1e29
SCALE = math.log2(math.e) / math.sqrt(HEAD_DIM)


def vmem():
    return pl.BlockSpec(memory_space=pltpu.VMEM)


def smem():
    return pl.BlockSpec(memory_space=pltpu.SMEM)


def rotate(values, cosine, sine):
    return values * cosine + pltpu.roll(values, HEAD_DIM // 2, 1) * sine


def project(first, pieces, w_ref):
    total = None
    for k, piece in enumerate(pieces):
        row = pl.multiple_of(lax.rem(first + k, N_TP) * FEATS, FEATS)
        part = jnp.dot(piece[...], w_ref[pl.ds(row, FEATS), :], preferred_element_type=jnp.float32)
        total = part if total is None else total + part
    return total


def kv_kernel(me_ref, *refs):
    pieces, (wk_ref, wv_ref, cos_ref, sin_ref, out_ref) = refs[:N_TP], refs[N_TP:]
    keys = project(me_ref[0], pieces, wk_ref)
    out_ref[:, :HEAD_DIM] = rotate(keys, cos_ref[...], sin_ref[...]).astype(jnp.bfloat16)
    out_ref[:, HEAD_DIM:] = project(me_ref[0], pieces, wv_ref).astype(jnp.bfloat16)


def q_kernel(me_ref, *refs):
    pieces, (wq_ref, cos_ref, sin_ref, out_ref) = refs[:N_TP], refs[N_TP:]
    queries = project(me_ref[0], pieces, wq_ref)
    for h in range(GROUP):
        cols = slice(h * HEAD_DIM, (h + 1) * HEAD_DIM)
        out_ref[:, cols] = rotate(queries[:, cols], cos_ref[...], sin_ref[...]).astype(jnp.bfloat16)


def attend_kernel(slot_ref, span_ref, bounds_ref, q_ref, kv_ref, out_ref, q_sc, m_sc, acc_sc):
    rows = GROUP * SPAN
    keys = STEP * SPAN
    ones = jnp.ones((keys, HEAD_DIM), jnp.bfloat16)

    def start_of(position):
        start = jnp.int32(0)
        for i in range(3):
            start = jnp.where(bounds_ref[i] <= position, bounds_ref[i], start)
        return start

    for b in range(ROWS // SPAN):
        for h in range(GROUP):
            q_sc[h * SPAN:(h + 1) * SPAN, :] = q_ref[b * SPAN:(b + 1) * SPAN, h * HEAD_DIM:(h + 1) * HEAD_DIM]
        m_sc[...] = jnp.full(m_sc.shape, LOWEST, jnp.float32)
        acc_sc[...] = jnp.zeros(acc_sc.shape, jnp.float32)
        own = span_ref[b]
        low = start_of(own * SPAN) // SPAN
        last_start = start_of(own * SPAN + SPAN - 1)
        count = (own - low) // STEP + 1
        plain_from = jnp.minimum((last_start - low * SPAN + keys - 1) // keys, count - 1)
        plain_from = jnp.maximum(plain_from, 0)
        row_pos = own * SPAN + lax.broadcasted_iota(jnp.int32, (rows, 1), 0) % SPAN
        row_start = jnp.zeros((rows, 1), jnp.int32)
        for i in range(3):
            row_start = jnp.where(bounds_ref[i] <= row_pos, bounds_ref[i], row_start)

        def step(i, masked):
            first = low + i * STEP
            parts = [
                kv_ref[pl.ds(pl.multiple_of(slot_ref[jnp.minimum(first + g, own)] * SPAN, SPAN), SPAN), :]
                for g in range(STEP)
            ]
            k = jnp.concatenate([p[:, :HEAD_DIM] for p in parts], axis=0)
            v = jnp.concatenate([p[:, HEAD_DIM:] for p in parts], axis=0)
            v = jnp.concatenate([v, ones], axis=1)
            scores = lax.dot_general(q_sc[...], k, (((1,), (1,)), ((), ())), preferred_element_type=jnp.float32) * SCALE
            if masked:
                key_pos = first * SPAN + lax.broadcasted_iota(jnp.int32, (rows, keys), 1)
                scores = jnp.where((key_pos <= row_pos) & (key_pos >= row_start), scores, MASKED)
            old = m_sc[...]
            new = jnp.maximum(old, jnp.max(scores, axis=1, keepdims=True))
            m_sc[...] = new
            weights = jnp.exp2(scores - jnp.concatenate([new] * STEP, axis=1)).astype(jnp.bfloat16)
            alpha = jnp.exp2(old - new)
            acc_sc[...] = acc_sc[...] * jnp.concatenate([alpha, alpha], axis=1) + jnp.dot(
                weights, v, preferred_element_type=jnp.float32
            )

        def loop(masked):
            def body(i, carry):
                step(i, masked)
                return carry

            return body

        lax.fori_loop(0, plain_from, loop(True), 0)
        lax.fori_loop(plain_from, count - 1, loop(False), 0)
        lax.fori_loop(count - 1, count, loop(True), 0)
        for h in range(GROUP):
            part = slice(h * SPAN, (h + 1) * SPAN)
            out_ref[b * SPAN:(b + 1) * SPAN, h * HEAD_DIM:(h + 1) * HEAD_DIM] = (
                acc_sc[part, :HEAD_DIM] / acc_sc[part, HEAD_DIM:]
            ).astype(jnp.bfloat16)


def out_kernel(ctx_ref, w_ref, out_ref):
    for j in range(N_TP):
        out_ref[j] = jnp.dot(
            ctx_ref[...], w_ref[:, j * FEATS:(j + 1) * FEATS], preferred_element_type=jnp.float32
        ).astype(jnp.bfloat16)


def call(kernel, shape, in_specs, scratch=(), vmem_mb=40, flops=0, nbytes=0):
    return pl.pallas_call(
        kernel,
        out_shape=shape,
        in_specs=in_specs,
        out_specs=vmem(),
        scratch_shapes=list(scratch),
        compiler_params=pltpu.CompilerParams(vmem_limit_bytes=vmem_mb << 20),
        cost_estimate=pl.CostEstimate(flops=flops, bytes_accessed=nbytes, transcendentals=0),
    )


def body(hidden_states, w_query, w_key, w_value, w_out, span_order, lengths):
    own_ctx = lax.axis_index("ctx")
    own_tp = lax.axis_index("tp")
    me = own_tp.reshape(1)

    with jax.named_scope("gather_hidden"):
        pieces = [hidden_states] + [
            lax.ppermute(hidden_states, "tp", [(i, (i - k) % N_TP) for i in range(N_TP)]) for k in range(1, N_TP)
        ]

    own_spans = lax.dynamic_slice_in_dim(span_order, own_ctx * 2, 2, 0)
    positions = (own_spans[:, None] * SPAN + jnp.arange(SPAN, dtype=jnp.int32)[None, :]).reshape(ROWS)
    half = HEAD_DIM // 2
    frequency = jnp.power(jnp.float32(ROPE_BASE), -(jnp.arange(half, dtype=jnp.float32) * (2.0 / HEAD_DIM)))
    angles = positions.astype(jnp.float32)[:, None] * frequency[None, :]
    cosine, sine = jnp.cos(angles), jnp.sin(angles)
    cosine = jnp.concatenate([cosine, cosine], axis=1)
    sine = jnp.concatenate([-sine, sine], axis=1)

    kv = call(
        kv_kernel,
        jax.ShapeDtypeStruct((ROWS, 2 * HEAD_DIM), jnp.bfloat16),
        [smem()] + [vmem()] * (N_TP + 4),
        flops=2 * ROWS * D * 2 * HEAD_DIM,
        nbytes=4 << 20,
    )(me, *pieces, w_key, w_value, cosine, sine)

    with jax.named_scope("gather_kv"):
        other = lax.ppermute(kv, "ctx", [(i, i ^ 2) for i in range(N_CTX)])
        column = jnp.concatenate([kv, other], axis=0)
        up = down = column
        rings = [column]
        for _ in range(3):
            up = lax.ppermute(up, "ctx", [(i, (i + 4) % N_CTX) for i in range(N_CTX)])
            down = lax.ppermute(down, "ctx", [(i, (i - 4) % N_CTX) for i in range(N_CTX)])
            rings += [up, down]
        up = lax.ppermute(up[:ROWS], "ctx", [(i, (i + 4) % N_CTX) for i in range(N_CTX)])
        down = lax.ppermute(down[ROWS:], "ctx", [(i, (i - 4) % N_CTX) for i in range(N_CTX)])
        rings += [up, down]
        flip = [(i, i ^ 1) for i in range(N_CTX)]
        mine = jnp.concatenate(rings, axis=0)
        theirs = [lax.ppermute(r, "ctx", flip) for r in rings]
        keys_values = jnp.concatenate([mine] + theirs, axis=0)

    base_z, low_bits = own_ctx // 4, own_ctx % 4
    offsets = jnp.array([0, 0, -1, -1, 1, 1, -2, -2, 2, 2, -3, -3, 3, 3, 4, 4], jnp.int32)
    flips = jnp.array([0, 2] * 8, jnp.int32)
    source = ((base_z + offsets) % 8) * 4 + (low_bits ^ flips)
    source = jnp.concatenate([source, source ^ 1])
    source_block = (source[:, None] * 2 + jnp.arange(2, dtype=jnp.int32)[None, :]).reshape(BLOCKS)
    slot_of_block = jnp.sum(
        jnp.where(source_block[None, :] == jnp.arange(BLOCKS, dtype=jnp.int32)[:, None], jnp.arange(BLOCKS, dtype=jnp.int32)[None, :], 0),
        axis=1,
    )
    slots = jnp.sum(
        jnp.where(span_order[None, :] == jnp.arange(BLOCKS, dtype=jnp.int32)[:, None], slot_of_block[None, :], 0), axis=1
    ).astype(jnp.int32)
    bounds = jnp.stack([lengths[0], lengths[0] + lengths[1], lengths[0] + lengths[1] + lengths[2]]).astype(jnp.int32)

    queries = call(
        q_kernel,
        jax.ShapeDtypeStruct((ROWS, GROUP * HEAD_DIM), jnp.bfloat16),
        [smem()] + [vmem()] * (N_TP + 3),
        flops=2 * ROWS * D * GROUP * HEAD_DIM,
        nbytes=6 << 20,
    )(me, *pieces, w_query, cosine, sine)

    context = call(
        attend_kernel,
        jax.ShapeDtypeStruct((ROWS, GROUP * HEAD_DIM), jnp.bfloat16),
        [smem()] * 3 + [vmem()] * 2,
        scratch=[
            pltpu.VMEM((GROUP * SPAN, HEAD_DIM), jnp.bfloat16),
            pltpu.VMEM((GROUP * SPAN, HEAD_DIM), jnp.float32),
            pltpu.VMEM((GROUP * SPAN, 2 * HEAD_DIM), jnp.float32),
        ],
        flops=4 * ROWS * GROUP * 4096 * HEAD_DIM,
        nbytes=5 << 20,
    )(slots, own_spans, bounds, queries, keys_values)

    partial = call(
        out_kernel,
        jax.ShapeDtypeStruct((N_TP, ROWS, FEATS), jnp.bfloat16),
        [vmem()] * 2,
        flops=2 * ROWS * GROUP * HEAD_DIM * D,
        nbytes=6 << 20,
    )(context, w_out)
    with jax.named_scope("scatter_out"):
        shares = lax.all_to_all(partial, "tp", 0, 0, tiled=True)
        return jnp.sum(shares.astype(jnp.float32), axis=0).astype(jnp.bfloat16)


def solution(mesh):
    in_specs = (
        P("ctx", "tp"),
        P(None, "tp"),
        P(None, "tp"),
        P(None, "tp"),
        P("tp", None),
        P(),
        P(),
    )
    return jax.shard_map(body, mesh=mesh, in_specs=in_specs, out_specs=P("ctx", "tp"), check_vma=False)
```

```python
import math

import jax
import jax.numpy as jnp
from jax import lax
from jax.experimental import pallas as pl
from jax.experimental.pallas import tpu as pltpu
from jax.sharding import PartitionSpec as P

HEADS = 32
KV_HEADS = 8
HEAD_DIM = 128
GROUP = HEADS // KV_HEADS
SPAN = 128
SEQ = 8192
D = 4096
N_CTX = 32
N_TP = 8
N_X = 4
FEATS = D // N_TP
ROWS = SEQ // N_CTX
HALF = ROWS // 2
BLOCKS = SEQ // SPAN
OWN_BLOCKS = ROWS // SPAN
STACK = GROUP * SPAN
STEP = 4
KEYS = STEP * SPAN
LIST = 40

ROPE_BASE = 500000.0
MASKED = -1e30
LOWEST = -1e29
SCALE = math.log2(math.e) / math.sqrt(HEAD_DIM)

CHUNKS = []
for entries in (
    [(0, 0), (0, 1), (-1, 0), (-1, 1), (1, 0), (1, 1)],
    [(-2, 0), (-2, 1), (2, 0), (2, 1)],
    [(-3, 0), (-3, 1), (3, 0), (3, 1)],
    [(4, 0), (4, 1)],
):
    CHUNKS.append([(k, y, core) for core in (0, 1) for k, y in entries])
FIRST_SLOT = [0]
for chunk in CHUNKS:
    FIRST_SLOT.append(FIRST_SLOT[-1] + OWN_BLOCKS * len(chunk))
N_LISTS = len(CHUNKS) * OWN_BLOCKS


def vmem():
    return pl.BlockSpec(memory_space=pltpu.VMEM)


def smem():
    return pl.BlockSpec(memory_space=pltpu.SMEM)


def call(kernel, shapes, in_specs, out_specs=None, scratch=(), vmem_mb=32, flops=0, nbytes=0):
    many = isinstance(shapes, (list, tuple))
    if out_specs is None:
        out_specs = [vmem() for _ in shapes] if many else vmem()
    return pl.pallas_call(
        kernel,
        out_shape=shapes,
        in_specs=in_specs,
        out_specs=out_specs,
        scratch_shapes=list(scratch),
        compiler_params=pltpu.CompilerParams(vmem_limit_bytes=vmem_mb << 20),
        cost_estimate=pl.CostEstimate(flops=flops, bytes_accessed=nbytes, transcendentals=0),
    )


def struct(shape, dtype=jnp.bfloat16):
    return jax.ShapeDtypeStruct(shape, dtype)


def member(me, dx, flip):
    x, y = me // 2, me % 2
    return ((x + dx + N_X) % N_X) * 2 + (y + flip) % 2


def tp_pairs(dx, flip):
    return [(t, ((t // 2 + dx) % N_X) * 2 + ((t % 2) ^ flip)) for t in range(N_TP)]


def send(rows, dx, flip):
    return lax.ppermute(rows, "tp", tp_pairs(dx, flip))


FLIP_CORE = [(i, i ^ 1) for i in range(N_CTX)]
FLIP_Y = [(i, i ^ 2) for i in range(N_CTX)]
UP_Z = [(i, (i + 4) % N_CTX) for i in range(N_CTX)]
DOWN_Z = [(i, (i - 4) % N_CTX) for i in range(N_CTX)]


def start_of(bounds, position):
    start = jnp.int32(0)
    for bound in bounds:
        start = jnp.where(bound <= position, bound, start)
    return start


def plan_kernel(span_ref, len_ref, ctx_ref, slot_out, pos_out, meta_out, slot_sc, count_sc):
    ctx = ctx_ref[0]
    z, y, core = ctx // 4, (ctx // 2) % 2, ctx % 2
    slot = 0
    for chunk in CHUNKS:
        for k, fy, fc in chunk:
            source = ((z + k + 8) % 8) * 4 + ((y + fy) % 2) * 2 + (core + fc) % 2
            for h in range(OWN_BLOCKS):
                slot_sc[span_ref[source * OWN_BLOCKS + h]] = slot
                slot += 1
    one = len_ref[0]
    two = one + len_ref[1]
    three = two + len_ref[2]
    bounds = (one, two, three)
    for i in range(3):
        meta_out[2 * N_LISTS + i] = bounds[i]
    for i in range(N_LISTS):
        count_sc[i] = 0
    for b in range(OWN_BLOCKS):
        own = span_ref[ctx * OWN_BLOCKS + b]
        meta_out[2 * N_LISTS + 3 + b] = own
        low = start_of(bounds, own * SPAN) // SPAN
        plain = jnp.minimum((start_of(bounds, own * SPAN + SPAN - 1) + SPAN - 1) // SPAN, own)

        def add(p):
            s = slot_sc[p]
            c = jnp.int32(0)
            base = jnp.int32(0)
            for first in FIRST_SLOT[1:-1]:
                c = c + jnp.where(s >= first, 1, 0)
                base = jnp.where(s >= first, first, base)
            which = c * OWN_BLOCKS + b
            n = count_sc[which]
            slot_out[which * LIST + n] = s - base
            pos_out[which * LIST + n] = p
            count_sc[which] = n + 1

        def body(p, carry):
            add(p)
            return carry

        lax.fori_loop(jnp.maximum(plain, low), own, body, 0)
        for c in range(len(CHUNKS)):
            meta_out[2 * (c * OWN_BLOCKS + b) + 1] = count_sc[c * OWN_BLOCKS + b]
        lax.fori_loop(low, plain, body, 0)
        add(own)
        for c in range(len(CHUNKS)):
            which = c * OWN_BLOCKS + b
            n = count_sc[which]
            meta_out[2 * which] = n
            for g in range(STEP - 1):
                slot_out[which * LIST + n + g] = 0
                pos_out[which * LIST + n + g] = BLOCKS


def rotate(values, cosine, sine):
    return values * cosine + pltpu.roll(values, HEAD_DIM // 2, 1) * sine


def rows_of(me, w_ref, dx, flip):
    return w_ref[pl.ds(pl.multiple_of(member(me, dx, flip) * FEATS, FEATS), FEATS), :]


def project_near(me, refs, w_ref):
    total = None
    for (dx, flip), ref in zip(((0, 0), (0, 1), (-1, 0), (1, 0)), refs):
        part = jnp.dot(ref[...], rows_of(me, w_ref, dx, flip), preferred_element_type=jnp.float32)
        total = part if total is None else total + part
    return total


def project_far(me, refs, w_ref):
    left, right, beside, top, low = refs
    total = None
    for (dx, flip), a, b in (
        ((-1, 1), left[:HALF, :], beside[:HALF, :]),
        ((1, 1), beside[HALF:, :], right[:HALF, :]),
        ((2, 0), left[HALF:, :], right[HALF:, :]),
        ((2, 1), top[...], low[...]),
    ):
        part = jnp.dot(
            jnp.concatenate([a, b], axis=0), rows_of(me, w_ref, dx, flip), preferred_element_type=jnp.float32
        )
        total = part if total is None else total + part
    return total


def kv_near_kernel(me_ref, a, b, c, d, w_ref, out_ref):
    out_ref[...] = project_near(me_ref[0], (a, b, c, d), w_ref)


def kv_far_kernel(me_ref, a, b, c, d, e, near_ref, w_ref, cos_ref, sin_ref, out_ref):
    total = near_ref[...] + project_far(me_ref[0], (a, b, c, d, e), w_ref)
    out_ref[:, :HEAD_DIM] = rotate(total[:, :HEAD_DIM], cos_ref[...], sin_ref[...]).astype(jnp.bfloat16)
    out_ref[:, HEAD_DIM:] = total[:, HEAD_DIM:].astype(jnp.bfloat16)


def q_kernel(me_ref, *refs):
    pieces, (w_ref, cos_ref, sin_ref, out_ref) = refs[:9], refs[9:]
    queries = project_near(me_ref[0], pieces[:4], w_ref) + project_far(me_ref[0], pieces[4:], w_ref)
    for h in range(GROUP):
        turned = rotate(queries[:, h * HEAD_DIM:(h + 1) * HEAD_DIM], cos_ref[...], sin_ref[...]).astype(jnp.bfloat16)
        for b in range(OWN_BLOCKS):
            out_ref[b, h * SPAN:(h + 1) * SPAN, :] = turned[b * SPAN:(b + 1) * SPAN, :]


def attend_kernel(index, slot_ref, pos_ref, meta_ref, q_ref, kv_ref, *refs):
    first, last = index == 0, index == len(CHUNKS) - 1
    if first:
        m_ref, acc_ref = refs
        m_ref[...] = jnp.full(m_ref.shape, LOWEST, jnp.float32)
        acc_ref[...] = jnp.zeros(acc_ref.shape, jnp.float32)
    elif last:
        _, _, out_ref, m_ref, acc_ref = refs
    else:
        _, _, m_ref, acc_ref = refs
    if not first:
        m_ref[...] = refs[0][...]
        acc_ref[...] = refs[1][...]
    ones = jnp.ones((KEYS, HEAD_DIM), jnp.bfloat16)
    bounds = [meta_ref[2 * N_LISTS + i] for i in range(3)]

    for b in range(OWN_BLOCKS):
        which = index * OWN_BLOCKS + b
        own = meta_ref[2 * N_LISTS + 3 + b]
        count, plain = meta_ref[2 * which], meta_ref[2 * which + 1]
        row_pos = own * SPAN + lax.broadcasted_iota(jnp.int32, (SPAN, 1), 0)
        row_start = jnp.zeros((SPAN, 1), jnp.int32)
        for bound in bounds:
            row_start = jnp.where(bound <= row_pos, bound, row_start)

        def step(i, masked):
            at = which * LIST + i * STEP
            parts = [
                kv_ref[pl.ds(pl.multiple_of(slot_ref[at + g] * SPAN, SPAN), SPAN), :] for g in range(STEP)
            ]
            k = jnp.concatenate([p[:, :HEAD_DIM] for p in parts], axis=0)
            v = jnp.concatenate([p[:, HEAD_DIM:] for p in parts], axis=0)
            v = jnp.concatenate([v, ones], axis=1)
            if masked:
                lane = lax.broadcasted_iota(jnp.int32, (SPAN, SPAN), 1)
                key_pos = jnp.concatenate([pos_ref[at + g] * SPAN + lane for g in range(STEP)], axis=1)
                bias = jnp.where((key_pos <= row_pos) & (key_pos >= row_start), 0.0, MASKED)
                bias = jnp.concatenate([bias] * GROUP, axis=0)
            scores = lax.dot_general(
                q_ref[b], k, (((1,), (1,)), ((), ())), preferred_element_type=jnp.float32
            ) * SCALE
            if masked:
                scores = scores + bias
            old = m_ref[b]
            new = jnp.maximum(old, jnp.max(scores, axis=1, keepdims=True))
            m_ref[b] = new
            weights = jnp.exp2(scores - jnp.concatenate([new] * STEP, axis=1)).astype(jnp.bfloat16)
            alpha = jnp.exp2(old - new)
            acc_ref[b] = acc_ref[b] * jnp.concatenate([alpha, alpha], axis=1) + jnp.dot(
                weights, v, preferred_element_type=jnp.float32
            )

        def loop(masked):
            def body(i, carry):
                step(i, masked)
                return carry

            return body

        lax.fori_loop(0, plain // STEP, loop(False), 0)
        lax.fori_loop(plain // STEP, (count + STEP - 1) // STEP, loop(True), 0)
        if last:
            for h in range(GROUP):
                part = slice(h * SPAN, (h + 1) * SPAN)
                out_ref[b * SPAN:(b + 1) * SPAN, h * HEAD_DIM:(h + 1) * HEAD_DIM] = (
                    acc_ref[b, part, :HEAD_DIM] / acc_ref[b, part, HEAD_DIM:]
                ).astype(jnp.bfloat16)


def share(me, ctx_ref, w_ref, dx, flip):
    col = pl.multiple_of(member(me, dx, flip) * FEATS, FEATS)
    return jnp.dot(ctx_ref[...], w_ref[:, pl.ds(col, FEATS)], preferred_element_type=jnp.float32)


def far_kernel(me_ref, ctx_ref, w_ref, top_ref, low_ref):
    total = share(me_ref[0], ctx_ref, w_ref, 2, 1).astype(jnp.bfloat16)
    top_ref[...] = total[:HALF]
    low_ref[...] = total[HALF:]


def middle_kernel(me_ref, ctx_ref, w_ref, beside_ref, left_ref, right_ref, across_ref):
    left = share(me_ref[0], ctx_ref, w_ref, -1, 1)
    right = share(me_ref[0], ctx_ref, w_ref, 1, 1)
    beside_ref[:HALF, :] = left[HALF:].astype(jnp.bfloat16)
    beside_ref[HALF:, :] = right[:HALF].astype(jnp.bfloat16)
    left_ref[...] = left[:HALF]
    right_ref[...] = right[HALF:]
    across_ref[...] = share(me_ref[0], ctx_ref, w_ref, 2, 0).astype(jnp.bfloat16)


def near_kernel(me_ref, ctx_ref, w_ref, own_ref, beside_ref, left_ref, right_ref):
    own_ref[...] = share(me_ref[0], ctx_ref, w_ref, 0, 0)
    beside_ref[...] = share(me_ref[0], ctx_ref, w_ref, 0, 1)
    left_ref[...] = share(me_ref[0], ctx_ref, w_ref, -1, 0)
    right_ref[...] = share(me_ref[0], ctx_ref, w_ref, 1, 0)


def add(a, b):
    return (a + b.astype(jnp.float32)).astype(jnp.bfloat16)


def body(hidden_states, w_query, w_key, w_value, w_out, span_order, lengths):
    own_ctx = lax.axis_index("ctx")
    me = lax.axis_index("tp").reshape(1)

    with jax.named_scope("gather_hidden"):
        beside = send(hidden_states, 0, 1)
        left, right = send(hidden_states, 1, 0), send(hidden_states, -1, 0)
        from_left = send(jnp.concatenate([beside[:HALF], left[:HALF]]), 1, 0)
        from_right = send(jnp.concatenate([beside[HALF:], right[HALF:]]), -1, 0)
        from_beside = send(jnp.concatenate([left[HALF:], right[:HALF]]), 0, 1)
        far_top = send(from_left[:HALF], 1, 0)
        far_low = send(from_right[:HALF], -1, 0)
    near = [hidden_states, beside, left, right]
    far = [from_left, from_right, from_beside, far_top, far_low]

    with jax.named_scope("tables"):
        own_spans = lax.dynamic_slice_in_dim(span_order, own_ctx * OWN_BLOCKS, OWN_BLOCKS, 0)
        positions = (own_spans[:, None] * SPAN + jnp.arange(SPAN, dtype=jnp.int32)[None, :]).reshape(ROWS)
        exponent = jnp.arange(HEAD_DIM // 2, dtype=jnp.float32) * (2.0 / HEAD_DIM)
        angles = positions.astype(jnp.float32)[:, None] * jnp.power(jnp.float32(ROPE_BASE), -exponent)[None, :]
        cosine, sine = jnp.cos(angles), jnp.sin(angles)
        cosine = jnp.concatenate([cosine, cosine], axis=1)
        sine = jnp.concatenate([-sine, sine], axis=1)
        w_kv = jnp.concatenate([w_key, w_value], axis=1)

    plan = call(
        plan_kernel,
        [
            struct((N_LISTS * LIST,), jnp.int32),
            struct((N_LISTS * LIST,), jnp.int32),
            struct((2 * N_LISTS + 3 + OWN_BLOCKS,), jnp.int32),
        ],
        [smem()] * 3,
        [smem()] * 3,
        scratch=[pltpu.SMEM((BLOCKS,), jnp.int32), pltpu.SMEM((N_LISTS,), jnp.int32)],
        nbytes=4 << 20,
    )(span_order, lengths, own_ctx.reshape(1))

    kv_near = call(
        kv_near_kernel,
        struct((ROWS, 2 * HEAD_DIM), jnp.float32),
        [smem()] + [vmem()] * 5,
        flops=2 * ROWS * D * HEAD_DIM,
        nbytes=3 << 20,
    )(me, *near, w_kv)
    kv = call(
        kv_far_kernel,
        struct((ROWS, 2 * HEAD_DIM)),
        [smem()] + [vmem()] * 9,
        flops=2 * ROWS * D * HEAD_DIM,
        nbytes=3 << 20,
    )(me, *far, kv_near, w_kv, cosine, sine)

    with jax.named_scope("gather_kv"):
        ring = lambda rows, pairs: lax.ppermute(rows, "ctx", pairs)
        column = jnp.concatenate([kv, ring(kv, FLIP_Y)], axis=0)
        ups, downs = [column], [column]
        for _ in range(3):
            ups.append(ring(ups[-1], UP_Z))
            downs.append(ring(downs[-1], DOWN_Z))
        last_up = ring(ups[-1][:ROWS], UP_Z)
        last_down = ring(downs[-1][ROWS:], DOWN_Z)
        chunks = []
        for held in ([column, ups[1], downs[1]], [ups[2], downs[2]], [ups[3], downs[3]], [last_up, last_down]):
            chunks.append(jnp.concatenate(held + [ring(rows, FLIP_CORE) for rows in held], axis=0))

    queries = call(
        q_kernel,
        struct((OWN_BLOCKS, STACK, HEAD_DIM)),
        [smem()] + [vmem()] * 12,
        flops=2 * ROWS * D * GROUP * HEAD_DIM,
        nbytes=6 << 20,
    )(me, *near, *far, w_query, cosine, sine)

    state_shapes = [
        struct((OWN_BLOCKS, STACK, HEAD_DIM), jnp.float32),
        struct((OWN_BLOCKS, STACK, 2 * HEAD_DIM), jnp.float32),
    ]
    state = []
    for index, chunk in enumerate(chunks):
        last = index == len(chunks) - 1
        state = call(
            lambda *refs, index=index: attend_kernel(index, *refs),
            struct((ROWS, GROUP * HEAD_DIM)) if last else state_shapes,
            [smem()] * 3 + [vmem()] * (2 + len(state)),
            scratch=[pltpu.VMEM(s.shape, s.dtype) for s in state_shapes] if last else (),
            flops=2 * ROWS * GROUP * chunk.shape[0] * HEAD_DIM,
            nbytes=4 << 20,
        )(*plan, queries, chunk, *state)
    context = state

    with jax.named_scope("scatter_out"):
        block = struct((ROWS, FEATS), jnp.float32)
        part = struct((HALF, FEATS), jnp.float32)
        top, low = call(
            far_kernel, [struct((HALF, FEATS))] * 2, [smem()] + [vmem()] * 2, flops=2 * ROWS * FEATS * FEATS, nbytes=1 << 20
        )(me, context, w_out)
        from_right, from_left = send(top, -1, 0), send(low, 1, 0)
        beside, left, right, across = call(
            middle_kernel,
            [struct((ROWS, FEATS)), part, part, struct((ROWS, FEATS))],
            [smem()] + [vmem()] * 2,
            flops=6 * ROWS * FEATS * FEATS,
            nbytes=3 << 20,
        )(me, context, w_out)
        from_beside = send(beside, 0, 1)
        own, own_beside, own_left, own_right = call(
            near_kernel, [block] * 4, [smem()] + [vmem()] * 2, flops=8 * ROWS * FEATS * FEATS, nbytes=4 << 20
        )(me, context, w_out)
        second_right = send(jnp.concatenate([add(left, from_right), across[:HALF]]), -1, 0)
        second_left = send(jnp.concatenate([add(right, from_left), across[HALF:]]), 1, 0)
        own_beside = add(own_beside, jnp.concatenate([second_right[:HALF], second_left[:HALF]]))
        own_left = add(own_left, jnp.concatenate([second_right[HALF:], from_beside[:HALF]]))
        own_right = add(own_right, jnp.concatenate([from_beside[HALF:], second_left[HALF:]]))
        arrived = [send(own_beside, 0, 1), send(own_left, -1, 0), send(own_right, 1, 0)]
        for rows in arrived:
            own = own + rows.astype(jnp.float32)
        return own.astype(jnp.bfloat16)


def solution(mesh):
    in_specs = (
        P("ctx", "tp"),
        P(None, "tp"),
        P(None, "tp"),
        P(None, "tp"),
        P("tp", None),
        P(),
        P(),
    )
    return jax.shard_map(body, mesh=mesh, in_specs=in_specs, out_specs=P("ctx", "tp"), check_vma=False)
```

```python
import math

import jax
import jax.numpy as jnp
from jax import lax
from jax.experimental import pallas as pl
from jax.experimental.pallas import tpu as pltpu
from jax.sharding import PartitionSpec as P

HEADS = 32
KV_HEADS = 8
HEAD_DIM = 128
GROUP = HEADS // KV_HEADS
SPAN = 128
SEQ = 8192
D = 4096
N_CTX = 32
N_TP = 8
N_X = 4
FEATS = D // N_TP
ROWS = SEQ // N_CTX
HALF = ROWS // 2
BLOCKS = SEQ // SPAN
OWN_BLOCKS = ROWS // SPAN
STACK = GROUP * SPAN
WIDE = 8
LIST = 32

ROPE_BASE = 500000.0
MASKED = -1e30
LOWEST = -1e29
SCALE = math.log2(math.e) / math.sqrt(HEAD_DIM)

CHUNKS = [
    [(0, 0), (0, 1), (-1, 0), (-1, 1), (1, 0), (1, 1)],
    [(-2, 0), (-2, 1), (2, 0), (2, 1)],
    [(-3, 0), (-3, 1), (3, 0), (3, 1)],
    [(4, 0), (4, 1)],
]
NARROW = [4, 4, 4, 2]
FIRST_SLOT = [0]
for chunk in CHUNKS:
    FIRST_SLOT.append(FIRST_SLOT[-1] + OWN_BLOCKS * len(chunk))
SIDES = 2
QUERY_BLOCKS = SIDES * OWN_BLOCKS
N_LISTS = len(CHUNKS) * QUERY_BLOCKS


def vmem():
    return pl.BlockSpec(memory_space=pltpu.VMEM)


def smem():
    return pl.BlockSpec(memory_space=pltpu.SMEM)


def call(kernel, shapes, in_specs, out_specs=None, scratch=(), vmem_mb=32, flops=0, nbytes=0):
    many = isinstance(shapes, (list, tuple))
    if out_specs is None:
        out_specs = [vmem() for _ in shapes] if many else vmem()
    return pl.pallas_call(
        kernel,
        out_shape=shapes,
        in_specs=in_specs,
        out_specs=out_specs,
        scratch_shapes=list(scratch),
        compiler_params=pltpu.CompilerParams(vmem_limit_bytes=vmem_mb << 20),
        cost_estimate=pl.CostEstimate(flops=flops, bytes_accessed=nbytes, transcendentals=0),
    )


def struct(shape, dtype=jnp.bfloat16):
    return jax.ShapeDtypeStruct(shape, dtype)


def member(me, dx, flip):
    x, y = me // 2, me % 2
    return ((x + dx + N_X) % N_X) * 2 + (y + flip) % 2


def tp_pairs(dx, flip):
    return [(t, ((t // 2 + dx) % N_X) * 2 + ((t % 2) ^ flip)) for t in range(N_TP)]


def send(rows, dx, flip):
    return lax.ppermute(rows, "tp", tp_pairs(dx, flip))


FLIP_CORE = [(i, i ^ 1) for i in range(N_CTX)]
FLIP_Y = [(i, i ^ 2) for i in range(N_CTX)]
UP_Z = [(i, (i + 4) % N_CTX) for i in range(N_CTX)]
DOWN_Z = [(i, (i - 4) % N_CTX) for i in range(N_CTX)]


def start_of(bounds, position):
    start = jnp.int32(0)
    for bound in bounds:
        start = jnp.where(bound <= position, bound, start)
    return start


def plan_kernel(span_ref, len_ref, ctx_ref, slot_out, pos_out, meta_out, slot_sc, count_sc):
    ctx = ctx_ref[0]
    z, y, core = ctx // 4, (ctx // 2) % 2, ctx % 2
    for p in range(BLOCKS):
        slot_sc[p] = -1
    slot = 0
    for chunk in CHUNKS:
        for k, fy in chunk:
            source = ((z + k + 8) % 8) * 4 + ((y + fy) % 2) * 2 + core
            for h in range(OWN_BLOCKS):
                slot_sc[span_ref[source * OWN_BLOCKS + h]] = slot
                slot += 1
    one = len_ref[0]
    two = one + len_ref[1]
    three = two + len_ref[2]
    bounds = (one, two, three)
    for i in range(3):
        meta_out[2 * N_LISTS + i] = bounds[i]
    for i in range(N_LISTS):
        count_sc[i] = 0
    for b in range(QUERY_BLOCKS):
        holder = ctx if b < OWN_BLOCKS else ctx + 1 - 2 * core
        own = span_ref[holder * OWN_BLOCKS + b % OWN_BLOCKS]
        meta_out[2 * N_LISTS + 3 + b] = own
        low = start_of(bounds, own * SPAN) // SPAN
        plain = jnp.minimum((start_of(bounds, own * SPAN + SPAN - 1) + SPAN - 1) // SPAN, own)

        def add(p):
            s = slot_sc[p]

            @pl.when(s >= 0)
            def _():
                c = jnp.int32(0)
                base = jnp.int32(0)
                for first in FIRST_SLOT[1:-1]:
                    c = c + jnp.where(s >= first, 1, 0)
                    base = jnp.where(s >= first, first, base)
                which = c * QUERY_BLOCKS + b
                n = count_sc[which]
                slot_out[which * LIST + n] = s - base
                pos_out[which * LIST + n] = p
                count_sc[which] = n + 1

        def body(p, carry):
            add(p)
            return carry

        lax.fori_loop(jnp.maximum(plain, low), own, body, 0)
        for c in range(len(CHUNKS)):
            meta_out[2 * (c * QUERY_BLOCKS + b) + 1] = count_sc[c * QUERY_BLOCKS + b]
        lax.fori_loop(low, plain, body, 0)
        add(own)
        for c in range(len(CHUNKS)):
            which = c * QUERY_BLOCKS + b
            n = count_sc[which]
            meta_out[2 * which] = n
            for g in range(NARROW[c] - 1):
                slot_out[which * LIST + n + g] = 0
                pos_out[which * LIST + n + g] = BLOCKS


def rotate(values, cosine, sine):
    return values * cosine + pltpu.roll(values, HEAD_DIM // 2, 1) * sine


def rows_of(me, w_ref, dx, flip):
    return w_ref[pl.ds(pl.multiple_of(member(me, dx, flip) * FEATS, FEATS), FEATS), :]


def project_near(me, refs, w_ref):
    total = None
    for (dx, flip), ref in zip(((0, 0), (0, 1), (-1, 0), (1, 0)), refs):
        part = jnp.dot(ref[...], rows_of(me, w_ref, dx, flip), preferred_element_type=jnp.float32)
        total = part if total is None else total + part
    return total


def project_far(me, refs, w_ref):
    left, right, beside, top, low = refs
    total = None
    for (dx, flip), a, b in (
        ((-1, 1), left[:HALF, :], beside[:HALF, :]),
        ((1, 1), beside[HALF:, :], right[:HALF, :]),
        ((2, 0), left[HALF:, :], right[HALF:, :]),
        ((2, 1), top[...], low[...]),
    ):
        part = jnp.dot(
            jnp.concatenate([a, b], axis=0), rows_of(me, w_ref, dx, flip), preferred_element_type=jnp.float32
        )
        total = part if total is None else total + part
    return total


def kv_near_kernel(me_ref, a, b, c, d, w_ref, out_ref):
    out_ref[...] = project_near(me_ref[0], (a, b, c, d), w_ref)


def kv_far_kernel(me_ref, a, b, c, d, e, near_ref, w_ref, cos_ref, sin_ref, out_ref):
    total = near_ref[...] + project_far(me_ref[0], (a, b, c, d, e), w_ref)
    out_ref[:, :HEAD_DIM] = rotate(total[:, :HEAD_DIM], cos_ref[...], sin_ref[...]).astype(jnp.bfloat16)
    out_ref[:, HEAD_DIM:] = total[:, HEAD_DIM:].astype(jnp.bfloat16)


def q_kernel(me_ref, *refs):
    pieces, (w_ref, cos_ref, sin_ref, out_ref) = refs[:9], refs[9:]
    queries = project_near(me_ref[0], pieces[:4], w_ref) + project_far(me_ref[0], pieces[4:], w_ref)
    for h in range(GROUP):
        turned = rotate(queries[:, h * HEAD_DIM:(h + 1) * HEAD_DIM], cos_ref[...], sin_ref[...]).astype(jnp.bfloat16)
        for b in range(OWN_BLOCKS):
            out_ref[b, h * SPAN:(h + 1) * SPAN, :] = turned[b * SPAN:(b + 1) * SPAN, :]


def attend_kernel(index, side, slot_ref, pos_ref, meta_ref, q_ref, kv_ref, *refs):
    narrow_width = NARROW[index]
    sends = side == 1 and index == len(CHUNKS) - 1
    if index == 0:
        m_ref, acc_ref = refs
        m_ref[...] = jnp.full(m_ref.shape, LOWEST, jnp.float32)
        acc_ref[...] = jnp.zeros(acc_ref.shape, jnp.float32)
    else:
        m_ref, acc_ref = refs[-2:]
        m_ref[...] = refs[0][...]
        acc_ref[...] = refs[1][...]
    bounds = [meta_ref[2 * N_LISTS + i] for i in range(3)]

    for b in range(OWN_BLOCKS):
        which = index * QUERY_BLOCKS + side * OWN_BLOCKS + b
        own = meta_ref[2 * N_LISTS + 3 + side * OWN_BLOCKS + b]
        count, plain = meta_ref[2 * which], meta_ref[2 * which + 1]
        row_pos = own * SPAN + lax.broadcasted_iota(jnp.int32, (SPAN, 1), 0)
        row_start = jnp.zeros((SPAN, 1), jnp.int32)
        for bound in bounds:
            row_start = jnp.where(bound <= row_pos, bound, row_start)

        def step(at, width, masked):
            parts = [
                kv_ref[pl.ds(pl.multiple_of(slot_ref[at + g] * SPAN, SPAN), SPAN), :] for g in range(width)
            ]
            k = jnp.concatenate([p[:, :HEAD_DIM] for p in parts], axis=0)
            v = jnp.concatenate([p[:, HEAD_DIM:] for p in parts], axis=0)
            v = jnp.concatenate([v, jnp.ones((width * SPAN, HEAD_DIM), jnp.bfloat16)], axis=1)
            heads = [slice(h * SPAN, (h + 1) * SPAN) for h in range(GROUP)]
            scores = [
                lax.dot_general(q_ref[b, h, :], k, (((1,), (1,)), ((), ())), preferred_element_type=jnp.float32) * SCALE
                for h in heads
            ]
            if masked:
                lane = lax.broadcasted_iota(jnp.int32, (SPAN, SPAN), 1)
                key_pos = jnp.concatenate([pos_ref[at + g] * SPAN + lane for g in range(width)], axis=1)
                bias = jnp.where((key_pos <= row_pos) & (key_pos >= row_start), 0.0, MASKED)
                scores = [s + bias for s in scores]
            old = [m_ref[b, h, :] for h in heads]
            new = [jnp.maximum(o, jnp.max(s, axis=1, keepdims=True)) for o, s in zip(old, scores)]
            weights = [
                jnp.exp2(s - jnp.concatenate([n] * width, axis=1)).astype(jnp.bfloat16) for s, n in zip(scores, new)
            ]
            for h, o, n, w in zip(heads, old, new, weights):
                m_ref[b, h, :] = n
                alpha = jnp.exp2(o - n)
                acc_ref[b, h, :] = acc_ref[b, h, :] * jnp.concatenate([alpha, alpha], axis=1) + jnp.dot(
                    w, v, preferred_element_type=jnp.float32
                )

        def wide(i, carry):
            step(which * LIST + i * WIDE, WIDE, False)
            return carry

        def narrow(i, carry):
            step(which * LIST + plain // WIDE * WIDE + i * narrow_width, narrow_width, True)
            return carry

        lax.fori_loop(0, plain // WIDE, wide, 0)
        lax.fori_loop(0, (count - plain // WIDE * WIDE + narrow_width - 1) // narrow_width, narrow, 0)
        if sends:
            rows_ref, stats_ref = refs[2:4]
            for h in range(GROUP):
                part = slice(h * SPAN, (h + 1) * SPAN)
                g = b * GROUP + h
                total = acc_ref[b, part, HEAD_DIM:]
                mean = acc_ref[b, part, :HEAD_DIM] / jnp.where(total > 0.0, total, 1.0)
                rows_ref[b, part, :] = mean.astype(jnp.bfloat16)
                stats_ref[g:g + 1, :] = jnp.sum(jnp.where(diagonal(), m_ref[b, part, :], 0.0), axis=0, keepdims=True)
                g += QUERY_BLOCKS * GROUP // SIDES
                stats_ref[g:g + 1, :] = jnp.sum(jnp.where(diagonal(), total, 0.0), axis=0, keepdims=True)


def diagonal():
    return lax.broadcasted_iota(jnp.int32, (SPAN, SPAN), 0) == lax.broadcasted_iota(jnp.int32, (SPAN, SPAN), 1)


def merge_kernel(m_ref, acc_ref, rows_ref, stats_ref, out_ref):
    for b in range(OWN_BLOCKS):
        for h in range(GROUP):
            part = slice(h * SPAN, (h + 1) * SPAN)
            g = b * GROUP + h
            column = lambda i: jnp.sum(jnp.where(diagonal(), stats_ref[i:i + 1, :], 0.0), axis=1, keepdims=True)
            their_high, their_total = column(g), column(g + OWN_BLOCKS * GROUP)
            high = m_ref[b, part, :]
            top = jnp.maximum(high, their_high)
            mine = jnp.exp2(high - top)
            theirs = jnp.exp2(their_high - top) * their_total
            summed = acc_ref[b, part, :HEAD_DIM] * mine + rows_ref[b, part, :].astype(jnp.float32) * theirs
            total = acc_ref[b, part, HEAD_DIM:] * mine + theirs
            out_ref[b * SPAN:(b + 1) * SPAN, h * HEAD_DIM:(h + 1) * HEAD_DIM] = (summed / total).astype(jnp.bfloat16)


def share(me, ctx_ref, w_ref, dx, flip):
    col = pl.multiple_of(member(me, dx, flip) * FEATS, FEATS)
    return jnp.dot(ctx_ref[...], w_ref[:, pl.ds(col, FEATS)], preferred_element_type=jnp.float32)


def far_kernel(me_ref, ctx_ref, w_ref, top_ref, low_ref):
    total = share(me_ref[0], ctx_ref, w_ref, 2, 1).astype(jnp.bfloat16)
    top_ref[...] = total[:HALF]
    low_ref[...] = total[HALF:]


def middle_kernel(me_ref, ctx_ref, w_ref, beside_ref, left_ref, right_ref, across_ref):
    left = share(me_ref[0], ctx_ref, w_ref, -1, 1)
    right = share(me_ref[0], ctx_ref, w_ref, 1, 1)
    beside_ref[:HALF, :] = left[HALF:].astype(jnp.bfloat16)
    beside_ref[HALF:, :] = right[:HALF].astype(jnp.bfloat16)
    left_ref[...] = left[:HALF]
    right_ref[...] = right[HALF:]
    across_ref[...] = share(me_ref[0], ctx_ref, w_ref, 2, 0).astype(jnp.bfloat16)


def near_kernel(me_ref, ctx_ref, w_ref, own_ref, beside_ref, left_ref, right_ref):
    own_ref[...] = share(me_ref[0], ctx_ref, w_ref, 0, 0)
    beside_ref[...] = share(me_ref[0], ctx_ref, w_ref, 0, 1)
    left_ref[...] = share(me_ref[0], ctx_ref, w_ref, -1, 0)
    right_ref[...] = share(me_ref[0], ctx_ref, w_ref, 1, 0)


def add(a, b):
    return (a + b.astype(jnp.float32)).astype(jnp.bfloat16)


def body(hidden_states, w_query, w_key, w_value, w_out, span_order, lengths):
    own_ctx = lax.axis_index("ctx")
    me = lax.axis_index("tp").reshape(1)

    with jax.named_scope("gather_hidden"):
        beside = send(hidden_states, 0, 1)
        left, right = send(hidden_states, 1, 0), send(hidden_states, -1, 0)
        from_left = send(jnp.concatenate([beside[:HALF], left[:HALF]]), 1, 0)
        from_right = send(jnp.concatenate([beside[HALF:], right[HALF:]]), -1, 0)
        from_beside = send(jnp.concatenate([left[HALF:], right[:HALF]]), 0, 1)
        far_top = send(from_left[:HALF], 1, 0)
        far_low = send(from_right[:HALF], -1, 0)
    near = [hidden_states, beside, left, right]
    far = [from_left, from_right, from_beside, far_top, far_low]

    with jax.named_scope("tables"):
        own_spans = lax.dynamic_slice_in_dim(span_order, own_ctx * OWN_BLOCKS, OWN_BLOCKS, 0)
        positions = (own_spans[:, None] * SPAN + jnp.arange(SPAN, dtype=jnp.int32)[None, :]).reshape(ROWS)
        exponent = jnp.arange(HEAD_DIM // 2, dtype=jnp.float32) * (2.0 / HEAD_DIM)
        angles = positions.astype(jnp.float32)[:, None] * jnp.power(jnp.float32(ROPE_BASE), -exponent)[None, :]
        cosine, sine = jnp.cos(angles), jnp.sin(angles)
        cosine = jnp.concatenate([cosine, cosine], axis=1)
        sine = jnp.concatenate([-sine, sine], axis=1)
        w_kv = jnp.concatenate([w_key, w_value], axis=1)

    plan = call(
        plan_kernel,
        [
            struct((N_LISTS * LIST,), jnp.int32),
            struct((N_LISTS * LIST,), jnp.int32),
            struct((2 * N_LISTS + 3 + OWN_BLOCKS,), jnp.int32),
        ],
        [smem()] * 3,
        [smem()] * 3,
        scratch=[pltpu.SMEM((BLOCKS,), jnp.int32), pltpu.SMEM((N_LISTS,), jnp.int32)],
        nbytes=4 << 20,
    )(span_order, lengths, own_ctx.reshape(1))

    kv_near = call(
        kv_near_kernel,
        struct((ROWS, 2 * HEAD_DIM), jnp.float32),
        [smem()] + [vmem()] * 5,
        flops=2 * ROWS * D * HEAD_DIM,
        nbytes=3 << 20,
    )(me, *near, w_kv)
    kv_near, plan = lax.optimization_barrier((kv_near, plan))
    kv = call(
        kv_far_kernel,
        struct((ROWS, 2 * HEAD_DIM)),
        [smem()] + [vmem()] * 9,
        flops=2 * ROWS * D * HEAD_DIM,
        nbytes=3 << 20,
    )(me, *far, kv_near, w_kv, cosine, sine)

    queries = call(
        q_kernel,
        struct((OWN_BLOCKS, STACK, HEAD_DIM)),
        [smem()] + [vmem()] * 12,
        flops=2 * ROWS * D * GROUP * HEAD_DIM,
        nbytes=6 << 20,
    )(me, *near, *far, w_query, cosine, sine)

    state_shapes = [
        struct((OWN_BLOCKS, STACK, HEAD_DIM), jnp.float32),
        struct((OWN_BLOCKS, STACK, 2 * HEAD_DIM), jnp.float32),
    ]
    sent_shapes = [struct((OWN_BLOCKS, STACK, HEAD_DIM)), struct((2 * OWN_BLOCKS * GROUP, SPAN), jnp.float32)]

    def attend(index, side, chunk, state):
        sends = side == 1 and index == len(CHUNKS) - 1
        return call(
            lambda *refs: attend_kernel(index, side, *refs),
            sent_shapes if sends else state_shapes,
            [smem()] * 3 + [vmem()] * (2 + len(state)),
            scratch=[pltpu.VMEM(s.shape, s.dtype) for s in state_shapes] if sends else (),
            flops=2 * ROWS * GROUP * chunk.shape[0] * HEAD_DIM,
            nbytes=4 << 20,
        )(*plan, (queries, their_queries)[side], chunk, *state)

    with jax.named_scope("gather_kv"):
        tie = lax.optimization_barrier
        their_queries = lax.ppermute(queries, "ctx", FLIP_CORE)
        column = jnp.concatenate([kv, lax.ppermute(kv, "ctx", FLIP_Y)], axis=0)
        column, their_queries = tie((column, their_queries))
        up, down = lax.ppermute(column, "ctx", UP_Z), lax.ppermute(column, "ctx", DOWN_Z)
        up2, down2 = lax.ppermute(up, "ctx", UP_Z), lax.ppermute(down, "ctx", DOWN_Z)
        chunk = jnp.concatenate([column, up, down], axis=0)
        theirs, mine = attend(0, 1, chunk, ()), attend(0, 0, chunk, ())
        up2, down2, theirs, mine = tie((up2, down2, theirs, mine))
        up3, down3 = lax.ppermute(up2, "ctx", UP_Z), lax.ppermute(down2, "ctx", DOWN_Z)
        chunk = jnp.concatenate([up2, down2], axis=0)
        theirs, mine = attend(1, 1, chunk, theirs), attend(1, 0, chunk, mine)
        up3, down3, theirs, mine = tie((up3, down3, theirs, mine))
        up4, down4 = lax.ppermute(up3[:ROWS], "ctx", UP_Z), lax.ppermute(down3[ROWS:], "ctx", DOWN_Z)
        chunk = jnp.concatenate([up3, down3], axis=0)
        theirs, mine = attend(2, 1, chunk, theirs), attend(2, 0, chunk, mine)
        up4, down4, theirs, mine = tie((up4, down4, theirs, mine))
        chunk = jnp.concatenate([up4, down4], axis=0)
        theirs = [lax.ppermute(sent, "ctx", FLIP_CORE) for sent in attend(3, 1, chunk, theirs)]
        mine = attend(3, 0, chunk, mine)
        context = call(
            merge_kernel, struct((ROWS, GROUP * HEAD_DIM)), [vmem()] * 4, flops=1 << 20, nbytes=2 << 20
        )(*mine, *theirs)

    with jax.named_scope("scatter_out"):
        block = struct((ROWS, FEATS), jnp.float32)
        part = struct((HALF, FEATS), jnp.float32)
        top, low = call(
            far_kernel, [struct((HALF, FEATS))] * 2, [smem()] + [vmem()] * 2, flops=2 * ROWS * FEATS * FEATS, nbytes=1 << 20
        )(me, context, w_out)
        context, top, low = lax.optimization_barrier((context, top, low))
        from_right, from_left = send(top, -1, 0), send(low, 1, 0)
        beside, left, right, across = call(
            middle_kernel,
            [struct((ROWS, FEATS)), part, part, struct((ROWS, FEATS))],
            [smem()] + [vmem()] * 2,
            flops=6 * ROWS * FEATS * FEATS,
            nbytes=3 << 20,
        )(me, context, w_out)
        from_beside = send(beside, 0, 1)
        own, own_beside, own_left, own_right = call(
            near_kernel, [block] * 4, [smem()] + [vmem()] * 2, flops=8 * ROWS * FEATS * FEATS, nbytes=4 << 20
        )(me, context, w_out)
        second_right = send(jnp.concatenate([add(left, from_right), across[:HALF]]), -1, 0)
        second_left = send(jnp.concatenate([add(right, from_left), across[HALF:]]), 1, 0)
        own_beside = add(own_beside, jnp.concatenate([second_right[:HALF], second_left[:HALF]]))
        own_left = add(own_left, jnp.concatenate([second_right[HALF:], from_beside[:HALF]]))
        own_right = add(own_right, jnp.concatenate([from_beside[HALF:], second_left[HALF:]]))
        arrived = [send(own_beside, 0, 1), send(own_left, -1, 0), send(own_right, 1, 0)]
        for rows in arrived:
            own = own + rows.astype(jnp.float32)
        return own.astype(jnp.bfloat16)


def solution(mesh):
    in_specs = (
        P("ctx", "tp"),
        P(None, "tp"),
        P(None, "tp"),
        P(None, "tp"),
        P("tp", None),
        P(),
        P(),
    )
    return jax.shard_map(body, mesh=mesh, in_specs=in_specs, out_specs=P("ctx", "tp"), check_vma=False)
```

```python
import math

import jax
import jax.numpy as jnp
from jax import lax
from jax.experimental import pallas as pl
from jax.experimental.pallas import tpu as pltpu
from jax.sharding import PartitionSpec as P

HEADS = 32
KV_HEADS = 8
HEAD_DIM = 128
GROUP = HEADS // KV_HEADS
SPAN = 128
SEQ = 8192
D = 4096
N_CTX = 32
N_TP = 8
N_X = 4
FEATS = D // N_TP
ROWS = SEQ // N_CTX
HALF = ROWS // 2
BLOCKS = SEQ // SPAN
OWN_BLOCKS = ROWS // SPAN
STACK = GROUP * SPAN
WIDE = 8
LIST = 32

ROPE_BASE = 500000.0
MASKED = -1e30
LOWEST = -1e29
SCALE = math.log2(math.e) / math.sqrt(HEAD_DIM)

CHUNKS = [
    [(0, 0), (0, 1), (-1, 0), (-1, 1), (1, 0), (1, 1)],
    [(-2, 0), (-2, 1), (2, 0), (2, 1)],
    [(-3, 0), (-3, 1), (3, 0), (3, 1)],
    [(4, 0), (4, 1)],
]
NARROW = [4, 4, 4, 2]
FIRST_SLOT = [0]
for chunk in CHUNKS:
    FIRST_SLOT.append(FIRST_SLOT[-1] + OWN_BLOCKS * len(chunk))
SIDES = 2
QUERY_BLOCKS = SIDES * OWN_BLOCKS
N_LISTS = len(CHUNKS) * QUERY_BLOCKS


def vmem():
    return pl.BlockSpec(memory_space=pltpu.VMEM)


def smem():
    return pl.BlockSpec(memory_space=pltpu.SMEM)


def call(kernel, shapes, in_specs, out_specs=None, scratch=(), vmem_mb=32, flops=0, nbytes=0):
    many = isinstance(shapes, (list, tuple))
    if out_specs is None:
        out_specs = [vmem() for _ in shapes] if many else vmem()
    return pl.pallas_call(
        kernel,
        out_shape=shapes,
        in_specs=in_specs,
        out_specs=out_specs,
        scratch_shapes=list(scratch),
        compiler_params=pltpu.CompilerParams(vmem_limit_bytes=vmem_mb << 20),
        cost_estimate=pl.CostEstimate(flops=flops, bytes_accessed=nbytes, transcendentals=0),
    )


def struct(shape, dtype=jnp.bfloat16):
    return jax.ShapeDtypeStruct(shape, dtype)


def member(me, dx, flip):
    x, y = me // 2, me % 2
    return ((x + dx + N_X) % N_X) * 2 + (y + flip) % 2


def tp_pairs(dx, flip):
    return [(t, ((t // 2 + dx) % N_X) * 2 + ((t % 2) ^ flip)) for t in range(N_TP)]


def send(rows, dx, flip):
    return lax.ppermute(rows, "tp", tp_pairs(dx, flip))


FLIP_CORE = [(i, i ^ 1) for i in range(N_CTX)]
FLIP_Y = [(i, i ^ 2) for i in range(N_CTX)]
UP_Z = [(i, (i + 4) % N_CTX) for i in range(N_CTX)]
DOWN_Z = [(i, (i - 4) % N_CTX) for i in range(N_CTX)]


def start_of(bounds, position):
    start = jnp.int32(0)
    for bound in bounds:
        start = jnp.where(bound <= position, bound, start)
    return start


def plan_kernel(span_ref, len_ref, ctx_ref, slot_out, pos_out, meta_out, slot_sc, count_sc):
    ctx = ctx_ref[0]
    z, y, core = ctx // 4, (ctx // 2) % 2, ctx % 2
    for p in range(BLOCKS):
        slot_sc[p] = -1
    slot = 0
    for chunk in CHUNKS:
        for k, fy in chunk:
            source = ((z + k + 8) % 8) * 4 + ((y + fy) % 2) * 2 + core
            for h in range(OWN_BLOCKS):
                slot_sc[span_ref[source * OWN_BLOCKS + h]] = slot
                slot += 1
    one = len_ref[0]
    two = one + len_ref[1]
    three = two + len_ref[2]
    bounds = (one, two, three)
    for i in range(3):
        meta_out[2 * N_LISTS + i] = bounds[i]
    for i in range(N_LISTS):
        count_sc[i] = 0
    for b in range(QUERY_BLOCKS):
        holder = ctx if b < OWN_BLOCKS else ctx + 1 - 2 * core
        own = span_ref[holder * OWN_BLOCKS + b % OWN_BLOCKS]
        meta_out[2 * N_LISTS + 3 + b] = own
        low = start_of(bounds, own * SPAN) // SPAN
        plain = jnp.minimum((start_of(bounds, own * SPAN + SPAN - 1) + SPAN - 1) // SPAN, own)

        def add(p):
            s = slot_sc[p]

            @pl.when(s >= 0)
            def _():
                c = jnp.int32(0)
                base = jnp.int32(0)
                for first in FIRST_SLOT[1:-1]:
                    c = c + jnp.where(s >= first, 1, 0)
                    base = jnp.where(s >= first, first, base)
                which = c * QUERY_BLOCKS + b
                n = count_sc[which]
                slot_out[which * LIST + n] = s - base
                pos_out[which * LIST + n] = p
                count_sc[which] = n + 1

        def body(p, carry):
            add(p)
            return carry

        lax.fori_loop(jnp.maximum(plain, low), own, body, 0)
        for c in range(len(CHUNKS)):
            meta_out[2 * (c * QUERY_BLOCKS + b) + 1] = count_sc[c * QUERY_BLOCKS + b]
        lax.fori_loop(low, plain, body, 0)
        add(own)
        for c in range(len(CHUNKS)):
            which = c * QUERY_BLOCKS + b
            n = count_sc[which]
            meta_out[2 * which] = n
            for g in range(NARROW[c] - 1):
                slot_out[which * LIST + n + g] = 0
                pos_out[which * LIST + n + g] = BLOCKS


def rotate(values, cosine, sine):
    return values * cosine + pltpu.roll(values, HEAD_DIM // 2, 1) * sine


def rows_of(me, w_ref, dx, flip):
    return w_ref[pl.ds(pl.multiple_of(member(me, dx, flip) * FEATS, FEATS), FEATS), :]


def project_near(me, refs, w_ref):
    total = None
    for (dx, flip), ref in zip(((0, 0), (0, 1), (-1, 0), (1, 0)), refs):
        part = jnp.dot(ref[...], rows_of(me, w_ref, dx, flip), preferred_element_type=jnp.float32)
        total = part if total is None else total + part
    return total


def project_far(me, refs, w_ref):
    left, right, beside, top, low = refs
    total = None
    for (dx, flip), a, b in (
        ((-1, 1), left[:HALF, :], beside[:HALF, :]),
        ((1, 1), beside[HALF:, :], right[:HALF, :]),
        ((2, 0), left[HALF:, :], right[HALF:, :]),
        ((2, 1), top[...], low[...]),
    ):
        part = jnp.dot(
            jnp.concatenate([a, b], axis=0), rows_of(me, w_ref, dx, flip), preferred_element_type=jnp.float32
        )
        total = part if total is None else total + part
    return total


def kv_near_kernel(me_ref, a, b, c, d, w_ref, out_ref):
    out_ref[...] = project_near(me_ref[0], (a, b, c, d), w_ref)


def kv_far_kernel(me_ref, a, b, c, d, e, near_ref, w_ref, cos_ref, sin_ref, out_ref):
    total = near_ref[...] + project_far(me_ref[0], (a, b, c, d, e), w_ref)
    out_ref[:, :HEAD_DIM] = rotate(total[:, :HEAD_DIM], cos_ref[...], sin_ref[...]).astype(jnp.bfloat16)
    out_ref[:, HEAD_DIM:] = total[:, HEAD_DIM:].astype(jnp.bfloat16)


def q_kernel(me_ref, *refs):
    pieces, (w_ref, cos_ref, sin_ref, out_ref) = refs[:9], refs[9:]
    queries = project_near(me_ref[0], pieces[:4], w_ref) + project_far(me_ref[0], pieces[4:], w_ref)
    for h in range(GROUP):
        turned = rotate(queries[:, h * HEAD_DIM:(h + 1) * HEAD_DIM], cos_ref[...], sin_ref[...]).astype(jnp.bfloat16)
        for b in range(OWN_BLOCKS):
            out_ref[b, h * SPAN:(h + 1) * SPAN, :] = turned[b * SPAN:(b + 1) * SPAN, :]


def attend_kernel(index, side, slot_ref, pos_ref, meta_ref, q_ref, kv_ref, *refs):
    narrow_width = NARROW[index]
    has_wide = FIRST_SLOT[index + 1] - FIRST_SLOT[index] > WIDE
    sends = side == 1 and index == len(CHUNKS) - 1
    if index == 0:
        m_ref, acc_ref = refs
        m_ref[...] = jnp.full(m_ref.shape, LOWEST, jnp.float32)
        acc_ref[...] = jnp.zeros(acc_ref.shape, jnp.float32)
    else:
        m_ref, acc_ref = refs[-2:]
        m_ref[...] = refs[0][...]
        acc_ref[...] = refs[1][...]
    bounds = [meta_ref[2 * N_LISTS + i] for i in range(3)]

    def block(b, unused):
        which = index * QUERY_BLOCKS + side * OWN_BLOCKS + b
        own = meta_ref[2 * N_LISTS + 3 + side * OWN_BLOCKS + b]
        count, plain = meta_ref[2 * which], meta_ref[2 * which + 1]
        row_pos = own * SPAN + lax.broadcasted_iota(jnp.int32, (SPAN, 1), 0)
        row_start = jnp.zeros((SPAN, 1), jnp.int32)
        for bound in bounds:
            row_start = jnp.where(bound <= row_pos, bound, row_start)

        def step(at, width, masked):
            parts = [
                kv_ref[pl.ds(pl.multiple_of(slot_ref[at + g] * SPAN, SPAN), SPAN), :] for g in range(width)
            ]
            k = jnp.concatenate([p[:, :HEAD_DIM] for p in parts], axis=0)
            v = jnp.concatenate([p[:, HEAD_DIM:] for p in parts], axis=0)
            v = jnp.concatenate([v, jnp.ones((width * SPAN, HEAD_DIM), jnp.bfloat16)], axis=1)
            heads = [slice(h * SPAN, (h + 1) * SPAN) for h in range(GROUP)]
            scores = [
                lax.dot_general(q_ref[b, h, :], k, (((1,), (1,)), ((), ())), preferred_element_type=jnp.float32) * SCALE
                for h in heads
            ]
            if masked:
                lane = lax.broadcasted_iota(jnp.int32, (SPAN, SPAN), 1)
                key_pos = jnp.concatenate([pos_ref[at + g] * SPAN + lane for g in range(width)], axis=1)
                bias = jnp.where((key_pos <= row_pos) & (key_pos >= row_start), 0.0, MASKED)
                scores = [s + bias for s in scores]
            old = [m_ref[b, h, :] for h in heads]
            new = [jnp.maximum(o, jnp.max(s, axis=1, keepdims=True)) for o, s in zip(old, scores)]
            weights = [
                jnp.exp2(s - jnp.concatenate([n] * width, axis=1)).astype(jnp.bfloat16) for s, n in zip(scores, new)
            ]
            for h, o, n, w in zip(heads, old, new, weights):
                m_ref[b, h, :] = n
                alpha = jnp.exp2(o - n)
                acc_ref[b, h, :] = acc_ref[b, h, :] * jnp.concatenate([alpha, alpha], axis=1) + jnp.dot(
                    w, v, preferred_element_type=jnp.float32
                )

        def wide(i, carry):
            step(which * LIST + i * WIDE, WIDE, False)
            return carry

        done = plain // WIDE * WIDE if has_wide else 0

        def narrow(i, carry):
            step(which * LIST + done + i * narrow_width, narrow_width, True)
            return carry

        if has_wide:
            lax.fori_loop(0, plain // WIDE, wide, 0)
        lax.fori_loop(0, (count - done + narrow_width - 1) // narrow_width, narrow, 0)
        return unused

    lax.fori_loop(0, OWN_BLOCKS, block, 0)
    if sends:
        rows_ref, stats_ref = refs[2:4]
        for b in range(OWN_BLOCKS):
            for h in range(GROUP):
                part = slice(h * SPAN, (h + 1) * SPAN)
                g = b * GROUP + h
                total = acc_ref[b, part, HEAD_DIM:]
                mean = acc_ref[b, part, :HEAD_DIM] / jnp.where(total > 0.0, total, 1.0)
                rows_ref[b, part, :] = mean.astype(jnp.bfloat16)
                stats_ref[g:g + 1, :] = jnp.sum(jnp.where(diagonal(), m_ref[b, part, :], 0.0), axis=0, keepdims=True)
                g += QUERY_BLOCKS * GROUP // SIDES
                stats_ref[g:g + 1, :] = jnp.sum(jnp.where(diagonal(), total, 0.0), axis=0, keepdims=True)


def diagonal():
    return lax.broadcasted_iota(jnp.int32, (SPAN, SPAN), 0) == lax.broadcasted_iota(jnp.int32, (SPAN, SPAN), 1)


def merge_kernel(m_ref, acc_ref, rows_ref, stats_ref, out_ref):
    for b in range(OWN_BLOCKS):
        for h in range(GROUP):
            part = slice(h * SPAN, (h + 1) * SPAN)
            g = b * GROUP + h
            column = lambda i: jnp.sum(jnp.where(diagonal(), stats_ref[i:i + 1, :], 0.0), axis=1, keepdims=True)
            their_high, their_total = column(g), column(g + OWN_BLOCKS * GROUP)
            high = m_ref[b, part, :]
            top = jnp.maximum(high, their_high)
            mine = jnp.exp2(high - top)
            theirs = jnp.exp2(their_high - top) * their_total
            summed = acc_ref[b, part, :HEAD_DIM] * mine + rows_ref[b, part, :].astype(jnp.float32) * theirs
            total = acc_ref[b, part, HEAD_DIM:] * mine + theirs
            out_ref[b * SPAN:(b + 1) * SPAN, h * HEAD_DIM:(h + 1) * HEAD_DIM] = (summed / total).astype(jnp.bfloat16)


def share(me, ctx_ref, w_ref, dx, flip):
    col = pl.multiple_of(member(me, dx, flip) * FEATS, FEATS)
    return jnp.dot(ctx_ref[...], w_ref[:, pl.ds(col, FEATS)], preferred_element_type=jnp.float32)


def far_kernel(me_ref, ctx_ref, w_ref, top_ref, low_ref):
    total = share(me_ref[0], ctx_ref, w_ref, 2, 1).astype(jnp.bfloat16)
    top_ref[...] = total[:HALF]
    low_ref[...] = total[HALF:]


def middle_kernel(me_ref, ctx_ref, w_ref, beside_ref, left_ref, right_ref, across_ref):
    left = share(me_ref[0], ctx_ref, w_ref, -1, 1)
    right = share(me_ref[0], ctx_ref, w_ref, 1, 1)
    beside_ref[:HALF, :] = left[HALF:].astype(jnp.bfloat16)
    beside_ref[HALF:, :] = right[:HALF].astype(jnp.bfloat16)
    left_ref[...] = left[:HALF]
    right_ref[...] = right[HALF:]
    across_ref[...] = share(me_ref[0], ctx_ref, w_ref, 2, 0).astype(jnp.bfloat16)


def near_kernel(me_ref, ctx_ref, w_ref, own_ref, beside_ref, left_ref, right_ref):
    own_ref[...] = share(me_ref[0], ctx_ref, w_ref, 0, 0)
    beside_ref[...] = share(me_ref[0], ctx_ref, w_ref, 0, 1)
    left_ref[...] = share(me_ref[0], ctx_ref, w_ref, -1, 0)
    right_ref[...] = share(me_ref[0], ctx_ref, w_ref, 1, 0)


def add(a, b):
    return (a + b.astype(jnp.float32)).astype(jnp.bfloat16)


def body(hidden_states, w_query, w_key, w_value, w_out, span_order, lengths):
    own_ctx = lax.axis_index("ctx")
    me = lax.axis_index("tp").reshape(1)

    with jax.named_scope("gather_hidden"):
        beside = send(hidden_states, 0, 1)
        left, right = send(hidden_states, 1, 0), send(hidden_states, -1, 0)
        from_left = send(jnp.concatenate([beside[:HALF], left[:HALF]]), 1, 0)
        from_right = send(jnp.concatenate([beside[HALF:], right[HALF:]]), -1, 0)
        from_beside = send(jnp.concatenate([left[HALF:], right[:HALF]]), 0, 1)
        far_top = send(from_left[:HALF], 1, 0)
        far_low = send(from_right[:HALF], -1, 0)
    near = [hidden_states, beside, left, right]
    far = [from_left, from_right, from_beside, far_top, far_low]

    with jax.named_scope("tables"):
        own_spans = lax.dynamic_slice_in_dim(span_order, own_ctx * OWN_BLOCKS, OWN_BLOCKS, 0)
        positions = (own_spans[:, None] * SPAN + jnp.arange(SPAN, dtype=jnp.int32)[None, :]).reshape(ROWS)
        exponent = jnp.arange(HEAD_DIM // 2, dtype=jnp.float32) * (2.0 / HEAD_DIM)
        angles = positions.astype(jnp.float32)[:, None] * jnp.power(jnp.float32(ROPE_BASE), -exponent)[None, :]
        cosine, sine = jnp.cos(angles), jnp.sin(angles)
        cosine = jnp.concatenate([cosine, cosine], axis=1)
        sine = jnp.concatenate([-sine, sine], axis=1)
        w_kv = jnp.concatenate([w_key, w_value], axis=1)

    plan = call(
        plan_kernel,
        [
            struct((N_LISTS * LIST,), jnp.int32),
            struct((N_LISTS * LIST,), jnp.int32),
            struct((2 * N_LISTS + 3 + OWN_BLOCKS,), jnp.int32),
        ],
        [smem()] * 3,
        [smem()] * 3,
        scratch=[pltpu.SMEM((BLOCKS,), jnp.int32), pltpu.SMEM((N_LISTS,), jnp.int32)],
        nbytes=4 << 20,
    )(span_order, lengths, own_ctx.reshape(1))

    kv_near = call(
        kv_near_kernel,
        struct((ROWS, 2 * HEAD_DIM), jnp.float32),
        [smem()] + [vmem()] * 5,
        flops=2 * ROWS * D * HEAD_DIM,
        nbytes=3 << 20,
    )(me, *near, w_kv)
    kv_near, plan = lax.optimization_barrier((kv_near, plan))
    kv = call(
        kv_far_kernel,
        struct((ROWS, 2 * HEAD_DIM)),
        [smem()] + [vmem()] * 9,
        flops=2 * ROWS * D * HEAD_DIM,
        nbytes=3 << 20,
    )(me, *far, kv_near, w_kv, cosine, sine)

    queries = call(
        q_kernel,
        struct((OWN_BLOCKS, STACK, HEAD_DIM)),
        [smem()] + [vmem()] * 12,
        flops=2 * ROWS * D * GROUP * HEAD_DIM,
        nbytes=6 << 20,
    )(me, *near, *far, w_query, cosine, sine)

    state_shapes = [
        struct((OWN_BLOCKS, STACK, HEAD_DIM), jnp.float32),
        struct((OWN_BLOCKS, STACK, 2 * HEAD_DIM), jnp.float32),
    ]
    sent_shapes = [struct((OWN_BLOCKS, STACK, HEAD_DIM)), struct((2 * OWN_BLOCKS * GROUP, SPAN), jnp.float32)]

    def attend(index, side, chunk, state):
        sends = side == 1 and index == len(CHUNKS) - 1
        return call(
            lambda *refs: attend_kernel(index, side, *refs),
            sent_shapes if sends else state_shapes,
            [smem()] * 3 + [vmem()] * (2 + len(state)),
            scratch=[pltpu.VMEM(s.shape, s.dtype) for s in state_shapes] if sends else (),
            flops=2 * ROWS * GROUP * chunk.shape[0] * HEAD_DIM,
            nbytes=4 << 20,
        )(*plan, (queries, their_queries)[side], chunk, *state)

    with jax.named_scope("gather_kv"):
        tie = lax.optimization_barrier
        their_queries = lax.ppermute(queries, "ctx", FLIP_CORE)
        column = jnp.concatenate([kv, lax.ppermute(kv, "ctx", FLIP_Y)], axis=0)
        column, their_queries = tie((column, their_queries))
        up, down = lax.ppermute(column, "ctx", UP_Z), lax.ppermute(column, "ctx", DOWN_Z)
        up2, down2 = lax.ppermute(up, "ctx", UP_Z), lax.ppermute(down, "ctx", DOWN_Z)
        chunk = jnp.concatenate([column, up, down], axis=0)
        theirs, mine = attend(0, 1, chunk, ()), attend(0, 0, chunk, ())
        up2, down2, theirs, mine = tie((up2, down2, theirs, mine))
        up3, down3 = lax.ppermute(up2, "ctx", UP_Z), lax.ppermute(down2, "ctx", DOWN_Z)
        chunk = jnp.concatenate([up2, down2], axis=0)
        theirs, mine = attend(1, 1, chunk, theirs), attend(1, 0, chunk, mine)
        up3, down3, theirs, mine = tie((up3, down3, theirs, mine))
        up4, down4 = lax.ppermute(up3[:ROWS], "ctx", UP_Z), lax.ppermute(down3[ROWS:], "ctx", DOWN_Z)
        chunk = jnp.concatenate([up3, down3], axis=0)
        theirs, mine = attend(2, 1, chunk, theirs), attend(2, 0, chunk, mine)
        up4, down4, theirs, mine = tie((up4, down4, theirs, mine))
        chunk = jnp.concatenate([up4, down4], axis=0)
        theirs = [lax.ppermute(sent, "ctx", FLIP_CORE) for sent in attend(3, 1, chunk, theirs)]
        mine = attend(3, 0, chunk, mine)
        context = call(
            merge_kernel, struct((ROWS, GROUP * HEAD_DIM)), [vmem()] * 4, flops=1 << 20, nbytes=2 << 20
        )(*mine, *theirs)

    with jax.named_scope("scatter_out"):
        block = struct((ROWS, FEATS), jnp.float32)
        part = struct((HALF, FEATS), jnp.float32)
        top, low = call(
            far_kernel, [struct((HALF, FEATS))] * 2, [smem()] + [vmem()] * 2, flops=2 * ROWS * FEATS * FEATS, nbytes=1 << 20
        )(me, context, w_out)
        context, top, low = lax.optimization_barrier((context, top, low))
        from_right, from_left = send(top, -1, 0), send(low, 1, 0)
        beside, left, right, across = call(
            middle_kernel,
            [struct((ROWS, FEATS)), part, part, struct((ROWS, FEATS))],
            [smem()] + [vmem()] * 2,
            flops=6 * ROWS * FEATS * FEATS,
            nbytes=3 << 20,
        )(me, context, w_out)
        from_beside = send(beside, 0, 1)
        own, own_beside, own_left, own_right = call(
            near_kernel, [block] * 4, [smem()] + [vmem()] * 2, flops=8 * ROWS * FEATS * FEATS, nbytes=4 << 20
        )(me, context, w_out)
        second_right = send(jnp.concatenate([add(left, from_right), across[:HALF]]), -1, 0)
        second_left = send(jnp.concatenate([add(right, from_left), across[HALF:]]), 1, 0)
        own_beside = add(own_beside, jnp.concatenate([second_right[:HALF], second_left[:HALF]]))
        own_left = add(own_left, jnp.concatenate([second_right[HALF:], from_beside[:HALF]]))
        own_right = add(own_right, jnp.concatenate([from_beside[HALF:], second_left[HALF:]]))
        arrived = [send(own_beside, 0, 1), send(own_left, -1, 0), send(own_right, 1, 0)]
        for rows in arrived:
            own = own + rows.astype(jnp.float32)
        return own.astype(jnp.bfloat16)


def solution(mesh):
    in_specs = (
        P("ctx", "tp"),
        P(None, "tp"),
        P(None, "tp"),
        P(None, "tp"),
        P("tp", None),
        P(),
        P(),
    )
    return jax.shard_map(body, mesh=mesh, in_specs=in_specs, out_specs=P("ctx", "tp"), check_vma=False)
```

```python
import math

import jax
import jax.numpy as jnp
from jax import lax
from jax.experimental import pallas as pl
from jax.experimental.pallas import tpu as pltpu
from jax.sharding import PartitionSpec as P

HEADS = 32
KV_HEADS = 8
HEAD_DIM = 128
GROUP = HEADS // KV_HEADS
SPAN = 128
SEQ = 8192
D = 4096
N_CTX = 32
N_TP = 8
N_X = 4
FEATS = D // N_TP
ROWS = SEQ // N_CTX
HALF = ROWS // 2
BLOCKS = SEQ // SPAN
OWN_BLOCKS = ROWS // SPAN
STACK = GROUP * SPAN
WIDE = 8
LIST = 32

ROPE_BASE = 500000.0
MASKED = -1e30
LOWEST = -1e29
SCALE = math.log2(math.e) / math.sqrt(HEAD_DIM)

CHUNKS = [
    [(0, 0), (0, 1), (-1, 0), (-1, 1), (1, 0), (1, 1)],
    [(-2, 0), (-2, 1), (2, 0), (2, 1)],
    [(-3, 0), (-3, 1), (3, 0), (3, 1)],
    [(4, 0), (4, 1)],
]
NARROW = [4, 4, 4, 4]
FIRST_SLOT = [0]
for chunk in CHUNKS:
    FIRST_SLOT.append(FIRST_SLOT[-1] + OWN_BLOCKS * len(chunk))
SIDES = 2
QUERY_BLOCKS = SIDES * OWN_BLOCKS
N_LISTS = len(CHUNKS) * QUERY_BLOCKS


def vmem():
    return pl.BlockSpec(memory_space=pltpu.VMEM)


def smem():
    return pl.BlockSpec(memory_space=pltpu.SMEM)


def call(kernel, shapes, in_specs, out_specs=None, scratch=(), vmem_mb=32, flops=0, nbytes=0):
    many = isinstance(shapes, (list, tuple))
    if out_specs is None:
        out_specs = [vmem() for _ in shapes] if many else vmem()
    return pl.pallas_call(
        kernel,
        out_shape=shapes,
        in_specs=in_specs,
        out_specs=out_specs,
        scratch_shapes=list(scratch),
        compiler_params=pltpu.CompilerParams(vmem_limit_bytes=vmem_mb << 20),
        cost_estimate=pl.CostEstimate(flops=flops, bytes_accessed=nbytes, transcendentals=0),
    )


def struct(shape, dtype=jnp.bfloat16):
    return jax.ShapeDtypeStruct(shape, dtype)


def member(me, dx, flip):
    x, y = me // 2, me % 2
    return ((x + dx + N_X) % N_X) * 2 + (y + flip) % 2


def tp_pairs(dx, flip):
    return [(t, ((t // 2 + dx) % N_X) * 2 + ((t % 2) ^ flip)) for t in range(N_TP)]


def send(rows, dx, flip):
    return lax.ppermute(rows, "tp", tp_pairs(dx, flip))


FLIP_CORE = [(i, i ^ 1) for i in range(N_CTX)]
FLIP_Y = [(i, i ^ 2) for i in range(N_CTX)]
UP_Z = [(i, (i + 4) % N_CTX) for i in range(N_CTX)]
DOWN_Z = [(i, (i - 4) % N_CTX) for i in range(N_CTX)]


def start_of(bounds, position):
    start = jnp.int32(0)
    for bound in bounds:
        start = jnp.where(bound <= position, bound, start)
    return start


def plan_kernel(span_ref, len_ref, ctx_ref, slot_out, pos_out, meta_out, slot_sc, count_sc):
    ctx = ctx_ref[0]
    z, y, core = ctx // 4, (ctx // 2) % 2, ctx % 2
    for p in range(BLOCKS):
        slot_sc[p] = -1
    slot = 0
    for chunk in CHUNKS:
        for k, fy in chunk:
            source = ((z + k + 8) % 8) * 4 + ((y + fy) % 2) * 2 + core
            for h in range(OWN_BLOCKS):
                slot_sc[span_ref[source * OWN_BLOCKS + h]] = slot
                slot += 1
    one = len_ref[0]
    two = one + len_ref[1]
    three = two + len_ref[2]
    bounds = (one, two, three)
    for i in range(3):
        meta_out[2 * N_LISTS + i] = bounds[i]
    for i in range(N_LISTS):
        count_sc[i] = 0
    for b in range(QUERY_BLOCKS):
        holder = ctx if b < OWN_BLOCKS else ctx + 1 - 2 * core
        own = span_ref[holder * OWN_BLOCKS + b % OWN_BLOCKS]
        meta_out[2 * N_LISTS + 3 + b] = own
        low = start_of(bounds, own * SPAN) // SPAN
        plain = jnp.minimum((start_of(bounds, own * SPAN + SPAN - 1) + SPAN - 1) // SPAN, own)

        def add(p):
            s = slot_sc[p]

            @pl.when(s >= 0)
            def _():
                c = jnp.int32(0)
                base = jnp.int32(0)
                for first in FIRST_SLOT[1:-1]:
                    c = c + jnp.where(s >= first, 1, 0)
                    base = jnp.where(s >= first, first, base)
                which = c * QUERY_BLOCKS + b
                n = count_sc[which]
                slot_out[which * LIST + n] = s - base
                pos_out[which * LIST + n] = p
                count_sc[which] = n + 1

        def body(p, carry):
            add(p)
            return carry

        lax.fori_loop(jnp.maximum(plain, low), own, body, 0)
        for c in range(len(CHUNKS)):
            meta_out[2 * (c * QUERY_BLOCKS + b) + 1] = count_sc[c * QUERY_BLOCKS + b]
        lax.fori_loop(low, plain, body, 0)
        add(own)
        for c in range(len(CHUNKS)):
            which = c * QUERY_BLOCKS + b
            n = count_sc[which]
            meta_out[2 * which] = n
            for g in range(NARROW[c]):
                slot_out[which * LIST + n + g] = 0
                pos_out[which * LIST + n + g] = BLOCKS


def rotate(values, cosine, sine):
    return values * cosine + pltpu.roll(values, HEAD_DIM // 2, 1) * sine


def rows_of(me, w_ref, dx, flip):
    return w_ref[pl.ds(pl.multiple_of(member(me, dx, flip) * FEATS, FEATS), FEATS), :]


def project_near(me, refs, w_ref):
    total = None
    for (dx, flip), ref in zip(((0, 0), (0, 1), (-1, 0), (1, 0)), refs):
        part = jnp.dot(ref[...], rows_of(me, w_ref, dx, flip), preferred_element_type=jnp.float32)
        total = part if total is None else total + part
    return total


def project_far(me, refs, w_ref):
    left, right, beside, top, low = refs
    total = None
    for (dx, flip), a, b in (
        ((-1, 1), left[:HALF, :], beside[:HALF, :]),
        ((1, 1), beside[HALF:, :], right[:HALF, :]),
        ((2, 0), left[HALF:, :], right[HALF:, :]),
        ((2, 1), top[...], low[...]),
    ):
        part = jnp.dot(
            jnp.concatenate([a, b], axis=0), rows_of(me, w_ref, dx, flip), preferred_element_type=jnp.float32
        )
        total = part if total is None else total + part
    return total


def kv_near_kernel(me_ref, a, b, c, d, w_ref, out_ref):
    out_ref[...] = project_near(me_ref[0], (a, b, c, d), w_ref)


def kv_far_kernel(me_ref, a, b, c, d, e, near_ref, w_ref, cos_ref, sin_ref, out_ref):
    total = near_ref[...] + project_far(me_ref[0], (a, b, c, d, e), w_ref)
    out_ref[:, :HEAD_DIM] = rotate(total[:, :HEAD_DIM], cos_ref[...], sin_ref[...]).astype(jnp.bfloat16)
    out_ref[:, HEAD_DIM:] = total[:, HEAD_DIM:].astype(jnp.bfloat16)


def q_kernel(me_ref, *refs):
    pieces, (w_ref, cos_ref, sin_ref, out_ref) = refs[:9], refs[9:]
    queries = project_near(me_ref[0], pieces[:4], w_ref) + project_far(me_ref[0], pieces[4:], w_ref)
    for h in range(GROUP):
        turned = rotate(queries[:, h * HEAD_DIM:(h + 1) * HEAD_DIM], cos_ref[...], sin_ref[...]).astype(jnp.bfloat16)
        for b in range(OWN_BLOCKS):
            out_ref[b, h * SPAN:(h + 1) * SPAN, :] = turned[b * SPAN:(b + 1) * SPAN, :]


def attend_kernel(index, side, slot_ref, pos_ref, meta_ref, q_ref, kv_ref, *refs):
    narrow_width = NARROW[index]
    has_wide = FIRST_SLOT[index + 1] - FIRST_SLOT[index] > WIDE
    sends = side == 1 and index == len(CHUNKS) - 1
    if index == 0:
        m_ref, acc_ref = refs
        m_ref[...] = jnp.full(m_ref.shape, LOWEST, jnp.float32)
        acc_ref[...] = jnp.zeros(acc_ref.shape, jnp.float32)
    else:
        m_ref, acc_ref = refs[-2:]
        m_ref[...] = refs[0][...]
        acc_ref[...] = refs[1][...]
    bounds = [meta_ref[2 * N_LISTS + i] for i in range(3)]

    def block(b, unused):
        which = index * QUERY_BLOCKS + side * OWN_BLOCKS + b
        own = meta_ref[2 * N_LISTS + 3 + side * OWN_BLOCKS + b]
        count, plain = meta_ref[2 * which], meta_ref[2 * which + 1]
        row_pos = own * SPAN + lax.broadcasted_iota(jnp.int32, (SPAN, 1), 0)
        row_start = jnp.zeros((SPAN, 1), jnp.int32)
        for bound in bounds:
            row_start = jnp.where(bound <= row_pos, bound, row_start)

        def step(at, width, masked):
            parts = [
                kv_ref[pl.ds(pl.multiple_of(slot_ref[at + g] * SPAN, SPAN), SPAN), :] for g in range(width)
            ]
            k = jnp.concatenate([p[:, :HEAD_DIM] for p in parts], axis=0)
            v = jnp.concatenate([p[:, HEAD_DIM:] for p in parts], axis=0)
            v = jnp.concatenate([v, jnp.ones((width * SPAN, HEAD_DIM), jnp.bfloat16)], axis=1)
            heads = [slice(h * SPAN, (h + 1) * SPAN) for h in range(GROUP)]
            scores = [
                lax.dot_general(q_ref[b, h, :], k, (((1,), (1,)), ((), ())), preferred_element_type=jnp.float32) * SCALE
                for h in heads
            ]
            if masked:
                lane = lax.broadcasted_iota(jnp.int32, (SPAN, SPAN), 1)
                key_pos = jnp.concatenate([pos_ref[at + g] * SPAN + lane for g in range(width)], axis=1)
                bias = jnp.where((key_pos <= row_pos) & (key_pos >= row_start), 0.0, MASKED)
                scores = [s + bias for s in scores]
            old = [m_ref[b, h, :] for h in heads]
            new = [jnp.maximum(o, jnp.max(s, axis=1, keepdims=True)) for o, s in zip(old, scores)]
            weights = [
                jnp.exp2(s - jnp.concatenate([n] * width, axis=1)).astype(jnp.bfloat16) for s, n in zip(scores, new)
            ]
            for h, o, n, w in zip(heads, old, new, weights):
                m_ref[b, h, :] = n
                alpha = jnp.exp2(o - n)
                acc_ref[b, h, :] = acc_ref[b, h, :] * jnp.concatenate([alpha, alpha], axis=1) + jnp.dot(
                    w, v, preferred_element_type=jnp.float32
                )

        def wide(i, carry):
            step(which * LIST + i * WIDE, WIDE, False)
            return carry

        done = plain // WIDE * WIDE if has_wide else 0

        def narrow(i, carry):
            step(which * LIST + done + i * narrow_width, narrow_width, True)
            return carry

        if index == len(CHUNKS) - 1:
            step(which * LIST, narrow_width, True)
            return unused
        if has_wide:
            lax.fori_loop(0, plain // WIDE, wide, 0)
        lax.fori_loop(0, (count - done + narrow_width - 1) // narrow_width, narrow, 0)
        return unused

    if index == len(CHUNKS) - 1:
        for b in range(OWN_BLOCKS):
            block(b, 0)
    else:
        lax.fori_loop(0, OWN_BLOCKS, block, 0)
    if sends:
        rows_ref, stats_ref = refs[2:4]
        for b in range(OWN_BLOCKS):
            for h in range(GROUP):
                part = slice(h * SPAN, (h + 1) * SPAN)
                g = b * GROUP + h
                total = acc_ref[b, part, HEAD_DIM:]
                mean = acc_ref[b, part, :HEAD_DIM] / jnp.where(total > 0.0, total, 1.0)
                rows_ref[b, part, :] = mean.astype(jnp.bfloat16)
                stats_ref[g:g + 1, :] = jnp.sum(jnp.where(diagonal(), m_ref[b, part, :], 0.0), axis=0, keepdims=True)
                g += QUERY_BLOCKS * GROUP // SIDES
                stats_ref[g:g + 1, :] = jnp.sum(jnp.where(diagonal(), total, 0.0), axis=0, keepdims=True)


def diagonal():
    return lax.broadcasted_iota(jnp.int32, (SPAN, SPAN), 0) == lax.broadcasted_iota(jnp.int32, (SPAN, SPAN), 1)


def merge_kernel(m_ref, acc_ref, rows_ref, stats_ref, out_ref):
    for b in range(OWN_BLOCKS):
        for h in range(GROUP):
            part = slice(h * SPAN, (h + 1) * SPAN)
            g = b * GROUP + h
            column = lambda i: jnp.sum(jnp.where(diagonal(), stats_ref[i:i + 1, :], 0.0), axis=1, keepdims=True)
            their_high, their_total = column(g), column(g + OWN_BLOCKS * GROUP)
            high = m_ref[b, part, :]
            top = jnp.maximum(high, their_high)
            mine = jnp.exp2(high - top)
            theirs = jnp.exp2(their_high - top) * their_total
            summed = acc_ref[b, part, :HEAD_DIM] * mine + rows_ref[b, part, :].astype(jnp.float32) * theirs
            total = acc_ref[b, part, HEAD_DIM:] * mine + theirs
            out_ref[b * SPAN:(b + 1) * SPAN, h * HEAD_DIM:(h + 1) * HEAD_DIM] = (summed / total).astype(jnp.bfloat16)


def share(me, ctx_ref, w_ref, dx, flip):
    col = pl.multiple_of(member(me, dx, flip) * FEATS, FEATS)
    return jnp.dot(ctx_ref[...], w_ref[:, pl.ds(col, FEATS)], preferred_element_type=jnp.float32)


def far_kernel(me_ref, ctx_ref, w_ref, top_ref, low_ref):
    total = share(me_ref[0], ctx_ref, w_ref, 2, 1).astype(jnp.bfloat16)
    top_ref[...] = total[:HALF]
    low_ref[...] = total[HALF:]


def middle_kernel(me_ref, ctx_ref, w_ref, beside_ref, left_ref, right_ref, across_ref):
    left = share(me_ref[0], ctx_ref, w_ref, -1, 1)
    right = share(me_ref[0], ctx_ref, w_ref, 1, 1)
    beside_ref[:HALF, :] = left[HALF:].astype(jnp.bfloat16)
    beside_ref[HALF:, :] = right[:HALF].astype(jnp.bfloat16)
    left_ref[...] = left[:HALF]
    right_ref[...] = right[HALF:]
    across_ref[...] = share(me_ref[0], ctx_ref, w_ref, 2, 0).astype(jnp.bfloat16)


def near_kernel(me_ref, ctx_ref, w_ref, own_ref, beside_ref, left_ref, right_ref):
    own_ref[...] = share(me_ref[0], ctx_ref, w_ref, 0, 0)
    beside_ref[...] = share(me_ref[0], ctx_ref, w_ref, 0, 1)
    left_ref[...] = share(me_ref[0], ctx_ref, w_ref, -1, 0)
    right_ref[...] = share(me_ref[0], ctx_ref, w_ref, 1, 0)


def add(a, b):
    return (a + b.astype(jnp.float32)).astype(jnp.bfloat16)


def body(hidden_states, w_query, w_key, w_value, w_out, span_order, lengths):
    own_ctx = lax.axis_index("ctx")
    me = lax.axis_index("tp").reshape(1)

    with jax.named_scope("gather_hidden"):
        beside = send(hidden_states, 0, 1)
        left, right = send(hidden_states, 1, 0), send(hidden_states, -1, 0)
        from_left = send(jnp.concatenate([beside[:HALF], left[:HALF]]), 1, 0)
        from_right = send(jnp.concatenate([beside[HALF:], right[HALF:]]), -1, 0)
        from_beside = send(jnp.concatenate([left[HALF:], right[:HALF]]), 0, 1)
        far_top = send(from_left[:HALF], 1, 0)
        far_low = send(from_right[:HALF], -1, 0)
    near = [hidden_states, beside, left, right]
    far = [from_left, from_right, from_beside, far_top, far_low]

    with jax.named_scope("tables"):
        own_spans = lax.dynamic_slice_in_dim(span_order, own_ctx * OWN_BLOCKS, OWN_BLOCKS, 0)
        positions = (own_spans[:, None] * SPAN + jnp.arange(SPAN, dtype=jnp.int32)[None, :]).reshape(ROWS)
        exponent = jnp.arange(HEAD_DIM // 2, dtype=jnp.float32) * (2.0 / HEAD_DIM)
        angles = positions.astype(jnp.float32)[:, None] * jnp.power(jnp.float32(ROPE_BASE), -exponent)[None, :]
        cosine, sine = jnp.cos(angles), jnp.sin(angles)
        cosine = jnp.concatenate([cosine, cosine], axis=1)
        sine = jnp.concatenate([-sine, sine], axis=1)
        w_kv = jnp.concatenate([w_key, w_value], axis=1)

    plan = call(
        plan_kernel,
        [
            struct((N_LISTS * LIST,), jnp.int32),
            struct((N_LISTS * LIST,), jnp.int32),
            struct((2 * N_LISTS + 3 + OWN_BLOCKS,), jnp.int32),
        ],
        [smem()] * 3,
        [smem()] * 3,
        scratch=[pltpu.SMEM((BLOCKS,), jnp.int32), pltpu.SMEM((N_LISTS,), jnp.int32)],
        nbytes=4 << 20,
    )(span_order, lengths, own_ctx.reshape(1))

    kv_near = call(
        kv_near_kernel,
        struct((ROWS, 2 * HEAD_DIM), jnp.float32),
        [smem()] + [vmem()] * 5,
        flops=2 * ROWS * D * HEAD_DIM,
        nbytes=3 << 20,
    )(me, *near, w_kv)
    kv_near, plan = lax.optimization_barrier((kv_near, plan))
    kv = call(
        kv_far_kernel,
        struct((ROWS, 2 * HEAD_DIM)),
        [smem()] + [vmem()] * 9,
        flops=2 * ROWS * D * HEAD_DIM,
        nbytes=3 << 20,
    )(me, *far, kv_near, w_kv, cosine, sine)

    queries = call(
        q_kernel,
        struct((OWN_BLOCKS, STACK, HEAD_DIM)),
        [smem()] + [vmem()] * 12,
        flops=2 * ROWS * D * GROUP * HEAD_DIM,
        nbytes=6 << 20,
    )(me, *near, *far, w_query, cosine, sine)

    state_shapes = [
        struct((OWN_BLOCKS, STACK, HEAD_DIM), jnp.float32),
        struct((OWN_BLOCKS, STACK, 2 * HEAD_DIM), jnp.float32),
    ]
    sent_shapes = [struct((OWN_BLOCKS, STACK, HEAD_DIM)), struct((2 * OWN_BLOCKS * GROUP, SPAN), jnp.float32)]

    def attend(index, side, chunk, state):
        sends = side == 1 and index == len(CHUNKS) - 1
        return call(
            lambda *refs: attend_kernel(index, side, *refs),
            sent_shapes if sends else state_shapes,
            [smem()] * 3 + [vmem()] * (2 + len(state)),
            scratch=[pltpu.VMEM(s.shape, s.dtype) for s in state_shapes] if sends else (),
            flops=2 * ROWS * GROUP * chunk.shape[0] * HEAD_DIM,
            nbytes=4 << 20,
        )(*plan, (queries, their_queries)[side], chunk, *state)

    with jax.named_scope("gather_kv"):
        tie = lax.optimization_barrier
        their_queries = lax.ppermute(queries, "ctx", FLIP_CORE)
        column = jnp.concatenate([kv, lax.ppermute(kv, "ctx", FLIP_Y)], axis=0)
        column, their_queries = tie((column, their_queries))
        up, down = lax.ppermute(column, "ctx", UP_Z), lax.ppermute(column, "ctx", DOWN_Z)
        up2, down2 = lax.ppermute(up, "ctx", UP_Z), lax.ppermute(down, "ctx", DOWN_Z)
        chunk = jnp.concatenate([column, up, down], axis=0)
        theirs, mine = attend(0, 1, chunk, ()), attend(0, 0, chunk, ())
        up2, down2, theirs, mine = tie((up2, down2, theirs, mine))
        up3, down3 = lax.ppermute(up2, "ctx", UP_Z), lax.ppermute(down2, "ctx", DOWN_Z)
        chunk = jnp.concatenate([up2, down2], axis=0)
        theirs, mine = attend(1, 1, chunk, theirs), attend(1, 0, chunk, mine)
        up3, down3, theirs, mine = tie((up3, down3, theirs, mine))
        up4, down4 = lax.ppermute(up3[:ROWS], "ctx", UP_Z), lax.ppermute(down3[ROWS:], "ctx", DOWN_Z)
        chunk = jnp.concatenate([up3, down3], axis=0)
        theirs, mine = attend(2, 1, chunk, theirs), attend(2, 0, chunk, mine)
        up4, down4, theirs, mine = tie((up4, down4, theirs, mine))
        chunk = jnp.concatenate([up4, down4], axis=0)
        theirs = [lax.ppermute(sent, "ctx", FLIP_CORE) for sent in attend(3, 1, chunk, theirs)]
        mine = attend(3, 0, chunk, mine)
        context = call(
            merge_kernel, struct((ROWS, GROUP * HEAD_DIM)), [vmem()] * 4, flops=1 << 20, nbytes=2 << 20
        )(*mine, *theirs)

    with jax.named_scope("scatter_out"):
        block = struct((ROWS, FEATS), jnp.float32)
        part = struct((HALF, FEATS), jnp.float32)
        top, low = call(
            far_kernel, [struct((HALF, FEATS))] * 2, [smem()] + [vmem()] * 2, flops=2 * ROWS * FEATS * FEATS, nbytes=1 << 20
        )(me, context, w_out)
        context, top, low = lax.optimization_barrier((context, top, low))
        from_right, from_left = send(top, -1, 0), send(low, 1, 0)
        beside, left, right, across = call(
            middle_kernel,
            [struct((ROWS, FEATS)), part, part, struct((ROWS, FEATS))],
            [smem()] + [vmem()] * 2,
            flops=6 * ROWS * FEATS * FEATS,
            nbytes=3 << 20,
        )(me, context, w_out)
        from_beside = send(beside, 0, 1)
        own, own_beside, own_left, own_right = call(
            near_kernel, [block] * 4, [smem()] + [vmem()] * 2, flops=8 * ROWS * FEATS * FEATS, nbytes=4 << 20
        )(me, context, w_out)
        second_right = send(jnp.concatenate([add(left, from_right), across[:HALF]]), -1, 0)
        second_left = send(jnp.concatenate([add(right, from_left), across[HALF:]]), 1, 0)
        own_beside = add(own_beside, jnp.concatenate([second_right[:HALF], second_left[:HALF]]))
        own_left = add(own_left, jnp.concatenate([second_right[HALF:], from_beside[:HALF]]))
        own_right = add(own_right, jnp.concatenate([from_beside[HALF:], second_left[HALF:]]))
        arrived = [send(own_beside, 0, 1), send(own_left, -1, 0), send(own_right, 1, 0)]
        for rows in arrived:
            own = own + rows.astype(jnp.float32)
        return own.astype(jnp.bfloat16)


def solution(mesh):
    in_specs = (
        P("ctx", "tp"),
        P(None, "tp"),
        P(None, "tp"),
        P(None, "tp"),
        P("tp", None),
        P(),
        P(),
    )
    return jax.shard_map(body, mesh=mesh, in_specs=in_specs, out_specs=P("ctx", "tp"), check_vma=False)
```
